512 devices in a mesh: dp: 32 (over z_hi, y, x), tensor: 16 (over z_lo, core).
Axes of the slice: x: 4, y: 4, z: 16 (z_hi: 2, z_lo: 8; z = z_hi * 8 + z_lo), core: 2. Of those that a mesh axis runs over, the one named last changes fastest.
Arguments:
- resid_src: bfloat16 [256, 4608], P('dp', 'tensor'), may hold values from -6 to 6
- enc_weight: bfloat16 [4608, 131072], P(None, ('dp', 'tensor')), may hold values from -0.09375 to 0.09375
- enc_bias: float32 [131072], P(('dp', 'tensor')), may hold values from -3 to 3
- active_ids: int32 [256, 64], replicated, may hold values from -1 to 131071, as said below
- dec_weight: bfloat16 [131072, 4608], P('dp', 'tensor'), may hold values from -0.75 to 0.75
- dec_bias: float32 [4608], P('tensor'), may hold values from -3 to 3
- segments: int32 [256], replicated, may hold values from 0 to 3, never falling along the last dimension, each value on 1 to 128 neighbouring positions
- attn_in_gain: float32 [4608], replicated, may hold values from 0.25 to 1.75
- post_gain: float32 [4608], replicated, may hold values from 0.25 to 1.75
- q_weight: bfloat16 [4608, 4096], P('dp', 'tensor'), may hold values from -1.41421356 to 1.41421356
- k_weight: bfloat16 [4608, 2048], P('dp', 'tensor'), may hold values from -0.09375 to 0.09375
- v_weight: bfloat16 [4608, 2048], P('dp', 'tensor'), may hold values from -0.09375 to 0.09375
- o_weight: bfloat16 [4096, 4608], P('tensor', 'dp'), may hold values from -0.09375 to 0.09375
Outputs:
- block_out: bfloat16 [256, 4608], P('dp', 'tensor')
The draws below stay inside these ranges and needn't reach their ends.
Inputs may be any that keep to these rules, and one draw needn't show every extreme that they name: `active_ids`: each row holds a number of latent ids, at least 32 and at most 64, followed by -1 in the remaining slots; ids may repeat within a row.
All inputs are finite; a program needn't handle non-finite values.
Results may differ from the reference program's by a relative error of at most 0.012.
The reference program's roundings to bfloat16 on the way (of `latent_act`, `selected`, `spliced`, `normed`, `queries` and `heads_out`) count: a program that leaves them out, or rounds other values in their place, can miss the bound.
Values may be sent and summed in bfloat16 or wider, within the bound.
A program may use at most 64 MiB of HBM per device.

```python
import math
import jax
import jax.numpy as jnp
import numpy as np
from jax import lax

D = 4608
HD = 128
HEADS_DEV = 2
SRC = 1
K = 64
HEADS = 32
KV_HEADS = 16
LAT = 131072
TOKENS = 256


def draw_active_ids(key, part):
    key = jax.random.fold_in(key, 11)
    id_key, live_key = jax.random.split(key)
    slot_index = jnp.arange(K, dtype=jnp.int32)[None, :]
    latent_ids = jax.random.randint(id_key, (TOKENS, K), 0, LAT, dtype=jnp.int32)
    live_count = jax.random.randint(live_key, (TOKENS, 1), K // 2, K + 1, dtype=jnp.int32)
    live_count = live_count.at[0, 0].set(K).at[TOKENS - 1, 0].set(K // 2)
    latent_ids = latent_ids.at[0, 0].set(LAT - 1)
    return jnp.where(slot_index < live_count, latent_ids, -1)


def draw_q_weight(key, part):
    key = jax.random.fold_in(key, 23)
    base_key, scale_key = jax.random.split(key)
    base = jnp.clip(jax.random.normal(base_key, (D, HEADS * HD), jnp.float32), -4.0, 4.0)
    head_scale = jnp.exp(jax.random.uniform(scale_key, (HEADS,), jnp.float32, 0.0, math.log(20.0)))
    column_scale = jnp.repeat(head_scale, HD)
    return (base * column_scale[None, :] * (1.0 / math.sqrt(D))).astype(jnp.bfloat16)


def shard_levels(own_key, shape, cuts, smallest, high):
    def one(position, parts):
        draws = jax.random.uniform(jax.random.fold_in(jax.random.fold_in(own_key, 6), position), (parts,), jnp.float32, smallest / len(cuts), high / len(cuts))
        return jnp.repeat(jnp.exp(draws), shape[position] // parts).reshape((-1,) + (1,) * (len(shape) - position - 1))

    loudness = one(*cuts[0])
    for cut in cuts[1:]:
        loudness = loudness * one(*cut)
    return loudness


def length_profile(count, total, reach, slope):
    loads = [(1 << 20) // math.isqrt(rank ** slope) + 1 for rank in range(2, count + 1)]
    spare, given = total - reach - (count - 1), [1] * (count - 1)
    while spare > 0:
        candidates = [i for i in range(count - 1) if given[i] < reach]
        mass, left = sum([loads[i] for i in candidates]), spare
        for i in candidates:
            addition = min(reach - given[i], max(1, left * loads[i] // mass), spare)
            given[i] = given[i] + addition
            spare = spare - addition
    return np.array([reach] + given)


def uneven_parts(stream_key, amount, total, most, lean):
    if amount == 2:
        one = jax.random.randint(stream_key, (), max(1, total - most), min(most, total - 1) + 1)
        return jnp.stack([one, total - one])
    sizes = jnp.asarray(length_profile(amount, total, most, lean), jnp.int32)
    pairs = (amount - 1) // 2
    donor, taker = sizes[1:1 + 2 * pairs:2], sizes[2:2 + 2 * pairs:2]
    margin = jnp.minimum(donor - 1, most - taker)
    shifted = jax.random.randint(jax.random.fold_in(stream_key, 1), (pairs,), 0, 1 << 20) % (margin + 1)
    sizes = sizes.at[1:1 + 2 * pairs:2].set(donor - shifted).at[2:2 + 2 * pairs:2].set(taker + shifted)
    return sizes[jax.random.permutation(jax.random.fold_in(stream_key, 2), amount)]


def noise(stream_key, extent, width, limit, shards=(), held_as=jnp.bfloat16):
    result = width * jax.random.normal(stream_key, extent, jnp.float32)
    if shards:
        result = result * shard_levels(stream_key, extent, shards, -0.22, 0.18)
    return jnp.clip(result, -limit, limit).astype(held_as)


def setup_inputs(seed: int = 0) -> dict:
    key_list = jax.random.split(jax.random.key(seed), 14)
    return {
        "resid_src": noise(key_list[0], (TOKENS, SRC * D), 1.0, 6.0, ((0, 32), (1, 16))),
        "enc_weight": noise(key_list[1], (SRC * D, LAT), (SRC * D) ** -0.5, 0.09375, ((1, 512),)),
        "enc_bias": noise(key_list[2], (LAT,), 0.5, 3.0, ((0, 512),), jnp.float32),
        "active_ids": draw_active_ids(jax.random.fold_in(key_list[13], 71), 0),
        "dec_weight": noise(key_list[4], (LAT, D), K ** -0.5, 0.75, ((0, 32), (1, 16))),
        "dec_bias": noise(key_list[5], (D,), 0.5, 3.0, ((0, 16),), jnp.float32),
        "segments": jnp.searchsorted(jnp.cumsum(uneven_parts(key_list[6], 4, TOKENS, TOKENS // 2, 0)), jnp.arange(TOKENS), side="right").astype(jnp.int32),
        "attn_in_gain": jnp.clip(1.0 + 0.15 * jax.random.normal(key_list[7], (D,), jnp.float32), 0.25, 1.75),
        "post_gain": jnp.clip(1.0 + 0.15 * jax.random.normal(key_list[8], (D,), jnp.float32), 0.25, 1.75),
        "q_weight": draw_q_weight(jax.random.fold_in(key_list[13], 71), 0),
        "k_weight": noise(key_list[10], (D, KV_HEADS * HD), D ** -0.5, 0.09375, ((0, 32), (1, 16))),
        "v_weight": noise(key_list[11], (D, KV_HEADS * HD), D ** -0.5, 0.09375, ((0, 32), (1, 16))),
        "o_weight": noise(key_list[12], (HEADS * HD, D), (HEADS * HD) ** -0.5, 0.09375, ((0, 16), (1, 32))),
    }


QUERY_SCALE = 144.0 ** (-0.5)
SOFT_CAP = 50.0

def norm_rows(values, gain):
    return values * lax.rsqrt(lax.optimization_barrier(jnp.mean(values * values, axis=-1, keepdims=True)) + 1e-06) * gain

def rotate(heads_in, positions):
    half_dim = heads_in.shape[-1] // 2
    freq_index = jnp.arange(half_dim, dtype=jnp.float32)
    inverse = jnp.exp(freq_index * (-2.0 * math.log(10000.0) / heads_in.shape[-1]))
    angles = positions[:, None, None] * inverse[None, None, :]
    cosine = jnp.cos(angles)
    sine = jnp.sin(angles)
    first = heads_in[..., :half_dim]
    second = heads_in[..., half_dim:]
    return jnp.concatenate([first * cosine - second * sine, second * cosine + first * sine], axis=-1)

def reference(resid_src, enc_weight, enc_bias, active_ids, dec_weight, dec_bias, segments, attn_in_gain, post_gain, q_weight, k_weight, v_weight, o_weight):
    pre_act = jnp.dot(resid_src, enc_weight, preferred_element_type=jnp.float32) + enc_bias
    latent_act = jnp.maximum(pre_act, 0.0).astype(jnp.bfloat16)
    live = active_ids >= 0
    row_ids = jnp.broadcast_to(jnp.arange(TOKENS, dtype=jnp.int32)[:, None], active_ids.shape)
    col_ids = jnp.where(live, active_ids, 0).astype(jnp.int32)
    counts = jnp.zeros((TOKENS, LAT), jnp.float32).at[row_ids, col_ids].add(live.astype(jnp.float32))
    selected = latent_act * counts.astype(jnp.bfloat16)
    recon = jnp.dot(selected, dec_weight, preferred_element_type=jnp.float32) + dec_bias
    spliced = recon.astype(jnp.bfloat16)
    resid_full = spliced.astype(jnp.float32)
    normed = norm_rows(resid_full, attn_in_gain).astype(jnp.bfloat16)
    tok_index = jnp.arange(TOKENS, dtype=jnp.int32)
    same_doc = segments[:, None] == segments[None, :]
    positions = lax.optimization_barrier(jnp.sum(same_doc & (tok_index[None, :] < tok_index[:, None]), axis=1)).astype(jnp.float32)
    queries = jnp.dot(normed, q_weight, preferred_element_type=jnp.float32).reshape(TOKENS, HEADS, HD)
    queries = (rotate(queries, positions) * QUERY_SCALE).astype(jnp.bfloat16)
    key_rows = jnp.dot(normed, k_weight, preferred_element_type=jnp.float32).reshape(TOKENS, KV_HEADS, HD)
    key_rows = rotate(key_rows, positions).astype(jnp.bfloat16)
    value_rows = jnp.dot(normed, v_weight, preferred_element_type=jnp.float32).astype(jnp.bfloat16).reshape(TOKENS, KV_HEADS, HD)
    key_wide = jnp.repeat(key_rows, HEADS_DEV, axis=1)
    value_wide = jnp.repeat(value_rows, HEADS_DEV, axis=1)
    scores = jnp.einsum('qhd,khd->hqk', queries.astype(jnp.float32), key_wide.astype(jnp.float32))
    capped = SOFT_CAP * jnp.tanh(scores / SOFT_CAP)
    allowed = same_doc & (tok_index[None, :] <= tok_index[:, None])
    weights = jnp.where(allowed[None], jnp.exp(capped), 0.0)
    totals = lax.optimization_barrier(jnp.sum(weights, axis=-1))
    rounded = lax.optimization_barrier(weights.astype(jnp.bfloat16))
    mixed = jnp.einsum('hqk,khd->hqd', rounded.astype(jnp.float32), value_wide.astype(jnp.float32))
    heads_out = (mixed / totals[:, :, None]).transpose(1, 0, 2).reshape(TOKENS, HEADS * HD).astype(jnp.bfloat16)
    attended = jnp.dot(heads_out, o_weight, preferred_element_type=jnp.float32)
    return (resid_full + norm_rows(attended, post_gain)).astype(jnp.bfloat16)
```

```python
import math

import jax
import jax.numpy as jnp
from jax import lax
from jax.experimental import pallas as pl
from jax.experimental.pallas import tpu as pltpu
from jax.sharding import PartitionSpec as P

QUERY_SCALE = 144.0 ** (-0.5)
SOFT_CAP = 50.0
EPS = 1e-06
MESH = pl.DeviceIdType.MESH
F32 = jnp.float32
BF16 = jnp.bfloat16


def kernel(
    NP, NT,
    resid, enc_hbm, enc_bias, ids_ref, dec_hbm, dec_bias, segs, gain_in, gain_post,
    q_hbm, k_hbm, v_hbm, o_hbm,
    out_ref,
    E, DEC, WQ, WK, WV, WO,
    COL, X, IDP, B, VS, VR, VG, S,
    RS, RR, ZS, ZR, SPF, SP, GIN, GPO, XS, XR, PS, PR, YS, YR, QR,
    CT, ST, MASK, HO, OS, OR, AS, AR, NR,
    lsem, ssem, rsem, r1b, r1c,
):
    T = 16 * NP
    R8 = 8 * NP
    NZ = NT // 2
    CH = resid.shape[1]
    HC = CH // 2
    D = NT * CH
    g = lax.axis_index("dp")
    s = lax.axis_index("tensor")
    zh = g // NP
    p = g % NP
    zl = s // 2
    c = s % 2

    def rcopy(src, dst, k, dp, tensor, rs=None):
        return pltpu.make_async_remote_copy(
            src_ref=src, dst_ref=dst, send_sem=ssem.at[k],
            recv_sem=rsem.at[k] if rs is None else rs,
            device_id={"dp": dp, "tensor": tensor}, device_id_type=MESH)

    def bulk(ref, n, sem):
        d = ref.at[pl.ds(0, n)]
        pltpu.make_async_copy(d, d, sem).wait()

    def to_plane(k, src, dst, rs=None):
        @pl.loop(1, NP)
        def _(j):
            q = (p + j) % NP
            rcopy(src(q), dst, k, zh * NP + q, s, rs).start()

    def to_tensor(k, src, dst):
        @pl.loop(1, NT)
        def _(j):
            q = (s + j) % NT
            rcopy(src(q), dst, k, g, q).start()

    loads = []
    for z in range(NZ):
        for h in range(2):
            row = pl.multiple_of((2 * z + (c if h == 0 else 1 - c)) * CH, 16)
            loads.append(pltpu.make_async_copy(
                enc_hbm.at[pl.ds(row, CH)], E.at[h, pl.ds(z * CH, CH)], lsem.at[len(loads)]))
    n_enc = len(loads)
    for a, b in ((dec_hbm, DEC), (q_hbm, WQ), (k_hbm, WK), (v_hbm, WV), (o_hbm, WO)):
        loads.append(pltpu.make_async_copy(a, b, lsem.at[len(loads)]))

    me_z = zh * NZ + zl
    @pl.loop(1, 2 * NZ)
    def _(j):
        z = (me_z + j) % (2 * NZ)
        rcopy(resid, COL.at[me_z], 0, (z // NZ) * NP + p, (z % NZ) * 2 + c).start()
    COL[me_z] = resid[...]
    for cp in loads:
        cp.start()

    a = ids_ref[...]
    IDP[:, :64] = a[:R8]
    IDP[:, 64:] = a[R8:]
    for j in range(NT):
        GIN[j:j + 1, :] = gain_in[:, j * CH:(j + 1) * CH]
        GPO[j:j + 1, :] = gain_post[:, j * CH:(j + 1) * CH]

    bulk(COL, 2 * NZ - 1, rsem.at[0])
    halves = []
    for h in range(2):
        halves.append(jnp.concatenate(
            [COL[h * NZ + z].astype(F32) for z in range(NZ)], axis=1))
    X[0, p] = jnp.concatenate(halves, axis=0).astype(BF16)
    to_plane(1, lambda q: X.at[0, p], X.at[0, p], r1b.at[p])
    rcopy(X.at[0, p], X.at[1, p], 2, g, s + 1 - 2 * c, r1c.at[p]).start()

    def tok(r):
        return ((r // 8) % 2) * R8 + (r // 16) * 8 + r % 8
    segc = jnp.broadcast_to(segs[...].astype(F32), (T, T)).T
    segc = jnp.concatenate(
        [segc[h * R8 + b * 8:h * R8 + b * 8 + 8] for b in range(NP) for h in range(2)], axis=0)
    tr = tok(lax.broadcasted_iota(jnp.int32, (T, T), 0))
    tc = tok(lax.broadcasted_iota(jnp.int32, (T, T), 1))
    same = segc == segc.T
    MASK[...] = jnp.where(same & (tc <= tr), 1.0, 0.0)
    pos = jnp.sum(jnp.where(same & (tc < tr), 1.0, 0.0), axis=1, keepdims=True)
    lane = lax.broadcasted_iota(jnp.int32, (1, 128), 1)
    inverse = jnp.exp((lane % 64).astype(F32) * (-2.0 * math.log(10000.0) / 128))
    ang = pos * inverse
    CT[...] = jnp.cos(ang)
    ST[...] = jnp.where(lane < 64, -1.0, 1.0) * jnp.sin(ang)

    def onehot(b):
        lo = (IDP[pl.ds(pl.multiple_of(b * 8, 8), 8), :] & 255).astype(F32).T
        cols = lax.broadcasted_iota(jnp.int32, (128, 256), 1).astype(F32)
        for i in range(8):
            B[b, pl.ds(i * 128, 128), :] = jnp.where(lo[:, i:i + 1] == cols, 1.0, 0.0).astype(BF16)

    onehot(0)
    @pl.loop(1, NP)
    def _(j):
        onehot(j)
        q = (p + NP - j) % NP
        pltpu.make_async_copy(X.at[0, q], X.at[0, q], r1b.at[q]).wait()
        rcopy(X.at[0, q], X.at[1, q], 2, g, s + 1 - 2 * c, r1c.at[q]).start()

    for cp in loads[:n_enc]:
        cp.wait()
    pre = jnp.dot(X[0].reshape(T, NZ * CH), E[0], preferred_element_type=F32)
    @pl.loop(0, NP)
    def _(q):
        pltpu.make_async_copy(X.at[1, q], X.at[1, q], r1c.at[q]).wait()
    pre = pre + jnp.dot(X[1].reshape(T, NZ * CH), E[1], preferred_element_type=F32)
    act = jnp.maximum(pre + enc_bias[...], 0.0).astype(BF16).astype(F32)

    act = act.reshape(NP, 2, 8, 256)
    a0 = act[:, 0].reshape(R8, 256)
    a1 = act[:, 1].reshape(R8, 256)
    rel = IDP[...] - (g * NT + s) * 256
    low = rel & 127
    left = lax.broadcasted_iota(jnp.int32, (R8, 128), 1) < 64

    def pick(h):
        return jnp.where(
            left,
            jnp.take_along_axis(a0[:, h * 128:(h + 1) * 128], low, axis=1),
            jnp.take_along_axis(a1[:, h * 128:(h + 1) * 128], low, axis=1))
    val = jnp.where(rel >= 128, pick(1), pick(0))
    val = jnp.where((rel >= 0) & (rel < 256), val, 0.0)
    VS[...] = val.reshape(NT, 8, 128)
    VR[s] = VS[s]
    to_tensor(3, lambda q: VS.at[q], VR.at[s])
    bulk(VR, NT - 1, rsem.at[3])
    VG[s] = jnp.sum(VR[...], axis=0)
    to_tensor(4, lambda q: VG.at[s], VG.at[s])
    bulk(VG, NT - 1, rsem.at[4])

    sub = lax.broadcasted_iota(jnp.int32, (8, 128), 0)
    lft = lax.broadcasted_iota(jnp.int32, (8, 128), 1) < 64
    @pl.loop(0, NP)
    def _(b):
        relb = IDP[pl.ds(pl.multiple_of(b * 8, 8), 8), :] - g * (NT * 256)
        vb = VG[b]
        hi = jnp.where(relb < 0, -1, relb >> 8)
        v0 = jnp.where(lft, vb, 0.0)
        v1 = vb - v0
        rows = []
        for h in range(NT):
            for vz in (v0, v1):
                d = jnp.where(hi == h, vz, 0.0)
                rows.append(jnp.concatenate([jnp.where(sub == i, d, 0.0) for i in range(8)], axis=1))
        lhs = jnp.concatenate(rows, axis=0).astype(BF16)
        sel = jnp.dot(lhs, B[b], preferred_element_type=F32).astype(BF16)
        S[:, pl.ds(pl.multiple_of(b * 16, 16), 16), :] = sel.reshape(NT, 16, 256)
    loads[n_enc].wait()
    rec = jnp.dot(S[0], DEC[pl.ds(0, 256), :], preferred_element_type=F32)
    for h in range(1, NT):
        rec = rec + jnp.dot(S[h], DEC[pl.ds(h * 256, 256), :], preferred_element_type=F32)
    RS[...] = rec.reshape(NP, 16, CH)
    RR[p] = RS[p]
    to_plane(5, lambda q: RS.at[q], RR.at[p])
    bulk(RR, NP - 1, rsem.at[5])
    ZS[...] = jnp.sum(RR[...], axis=0)
    zp = (1 - zh) * NP + p
    zc = rcopy(ZS, ZR, 6, zp, s)
    zc.start()
    zc.wait_recv()
    spl = (ZS[...] + ZR[...] + dec_bias[...]).astype(BF16)
    SPF[...] = spl.astype(F32).reshape(2, 8, CH)
    SP[s] = spl
    to_tensor(7, lambda q: SP.at[s], SP.at[s])
    for cp in loads[n_enc + 1:]:
        cp.wait()
    bulk(SP, NT - 1, rsem.at[7])

    ss = jnp.zeros((16, 1), F32)
    for j in range(NT):
        xj = SP[j].astype(F32)
        ss = ss + jnp.sum(xj * xj, axis=1, keepdims=True)
    rn = lax.rsqrt(ss / D + EPS)
    for j in range(NP // 2):
        cj = zh * (NP // 2) + j
        n = SP[cj].astype(F32) * rn * GIN[pl.ds(cj, 1), :]
        XS[2 * j] = n[:, :HC].astype(BF16)
        XS[2 * j + 1] = n[:, HC:].astype(BF16)
    XR[p] = XS[p]
    to_plane(8, lambda q: XS.at[q], XR.at[p])
    bulk(XR, NP - 1, rsem.at[8])
    xr = XR[...].reshape(T, HC)
    PS[:, :, 0:256] = jnp.dot(xr, WQ[...], preferred_element_type=F32).reshape(NP, 16, 256)
    PS[:, :, 256:384] = jnp.dot(xr, WK[...], preferred_element_type=F32).reshape(NP, 16, 128)
    PS[:, :, 384:512] = jnp.dot(xr, WV[...], preferred_element_type=F32).reshape(NP, 16, 128)
    PR[p] = PS[p]
    to_plane(9, lambda q: PS.at[q], PR.at[p])
    bulk(PR, NP - 1, rsem.at[9])
    YS[...] = jnp.sum(PR[...], axis=0)
    yc = rcopy(YS, YR, 10, zp, s)
    yc.start()
    yc.wait_recv()
    y = YS[...] + YR[...]
    mine = pl.ds(pl.multiple_of(p * 16, 16), 16)
    cosine, sine = CT[mine, :], ST[mine, :]

    def rot(x):
        return x * cosine + pltpu.roll(x, 64, 1) * sine
    QR[p] = jnp.concatenate(
        [rot(y[:, 0:128]) * QUERY_SCALE, rot(y[:, 128:256]) * QUERY_SCALE,
         rot(y[:, 256:384]), y[:, 384:512]], axis=1).astype(BF16)
    to_plane(11, lambda q: QR.at[p], QR.at[p])
    bulk(QR, NP - 1, rsem.at[11])

    kk = QR[:, :, 256:384].reshape(T, 128)
    vv = QR[:, :, 384:512].reshape(T, 128)
    for h in range(2):
        qq = QR[:, :, h * 128:(h + 1) * 128].reshape(T, 128)
        sc = lax.dot_general(qq, kk, (((1,), (1,)), ((), ())), preferred_element_type=F32)
        w = jnp.where(MASK[...] > 0.0, jnp.exp(SOFT_CAP * jnp.tanh(sc / SOFT_CAP)), 0.0)
        tot = jnp.sum(w, axis=1, keepdims=True)
        mixed = jnp.dot(w.astype(BF16), vv, preferred_element_type=F32)
        HO[:, h * 128:(h + 1) * 128] = (mixed / tot).astype(BF16)
    OS[...] = jnp.dot(HO[...], WO[...], preferred_element_type=F32).reshape(NT, 16, HC)
    OR[s] = OS[s]
    to_tensor(12, lambda q: OS.at[q], OR.at[s])
    bulk(OR, NT - 1, rsem.at[12])
    AS[...] = jnp.sum(OR[...], axis=0).reshape(2, 8, HC)

    slot = g % 2
    for z in range(2):
        here = (z * NP + s == g) & (g // 2 == s)

        @pl.when(here)
        def _():
            cp = pltpu.make_async_copy(AS.at[z], AR.at[slot], r1b.at[z])
            cp.start()
            cp.wait()

        @pl.when(jnp.logical_not(here))
        def _():
            rcopy(AS.at[z], AR.at[slot], 13 + z, z * NP + s, g // 2, r1c.at[slot]).start()
    for j in range(2):
        from_me = (2 * s + j == g) & (p == s)

        @pl.when(jnp.logical_not(from_me))
        def _():
            pltpu.make_async_copy(AR.at[j], AR.at[j], r1c.at[j]).wait()
    att = jnp.concatenate([AR[0], AR[1]], axis=1)
    NR[s] = jnp.broadcast_to(jnp.sum(att * att, axis=1, keepdims=True), (8, 128))
    to_tensor(15, lambda q: NR.at[s], NR.at[s])
    bulk(NR, NT - 1, rsem.at[15])
    tot = jnp.sum(NR[...], axis=0)[:, 0:1]
    post = att * lax.rsqrt(tot / D + EPS) * GPO[pl.ds(s, 1), :]
    out_ref[...] = (SPF[zh] + post).astype(BF16)

    bulk(COL, 2 * NZ - 1, ssem.at[0])
    bulk(X.at[0], NP - 1, ssem.at[1])
    bulk(X.at[0], NP, ssem.at[2])
    bulk(VS, NT - 1, ssem.at[3])
    bulk(VG, NT - 1, ssem.at[4])
    bulk(RS, NP - 1, ssem.at[5])
    zc.wait_send()
    bulk(SP, NT - 1, ssem.at[7])
    bulk(XS, NP - 1, ssem.at[8])
    bulk(PS, NP - 1, ssem.at[9])
    yc.wait_send()
    bulk(QR, NP - 1, ssem.at[11])
    bulk(OS, NT - 1, ssem.at[12])
    for z in range(2):
        here = (z * NP + s == g) & (g // 2 == s)

        @pl.when(jnp.logical_not(here))
        def _():
            pltpu.make_async_copy(AS.at[z], AS.at[z], ssem.at[13 + z]).wait()
    bulk(NR, NT - 1, ssem.at[15])


def local(mesh, resid, enc, enc_bias, ids, dec, dec_bias, segs, gin, gpo, qw, kw, vw, ow):
    NT = mesh.shape["tensor"]
    NP = mesh.shape["dp"] // 2
    assert NT == NP
    T, CH, NZ = 16 * NP, resid.shape[1], NT // 2
    HC = CH // 2
    V = pltpu.VMEM
    scratch = [
        V((2, NZ * CH, 256), BF16), V(dec.shape, BF16), V(qw.shape, BF16), V(kw.shape, BF16),
        V(vw.shape, BF16), V(ow.shape, BF16),
        V((2 * NZ, 8, CH), BF16), V((2, NP, 16, NZ * CH), BF16), V((8 * NP, 128), jnp.int32),
        V((NP, 1024, 256), BF16), V((NT, 8, 128), F32), V((NT, 8, 128), F32), V((NT, 8, 128), F32),
        V((NT, T, 256), BF16),
        V((NP, 16, CH), F32), V((NP, 16, CH), F32), V((16, CH), F32), V((16, CH), F32),
        V((2, 8, CH), F32), V((NT, 16, CH), BF16), V((NT, CH), F32), V((NT, CH), F32),
        V((NP, 16, HC), BF16), V((NP, 16, HC), BF16), V((NP, 16, 512), F32), V((NP, 16, 512), F32),
        V((16, 512), F32), V((16, 512), F32), V((NP, 16, 512), BF16),
        V((T, 128), F32), V((T, 128), F32), V((T, T), F32), V((T, 256), BF16),
        V((NT, 16, HC), F32), V((NT, 16, HC), F32), V((2, 8, HC), F32), V((2, 8, HC), F32),
        V((NT, 8, 128), F32),
        pltpu.SemaphoreType.DMA((2 * NZ + 5,)), pltpu.SemaphoreType.DMA((16,)),
        pltpu.SemaphoreType.DMA((16,)), pltpu.SemaphoreType.DMA((NP,)), pltpu.SemaphoreType.DMA((NP,)),
    ]
    vm = pl.BlockSpec(memory_space=V)
    hbm = pl.BlockSpec(memory_space=pl.ANY)
    return pl.pallas_call(
        lambda *refs: kernel(NP, NT, *refs),
        out_shape=jax.ShapeDtypeStruct((8, CH), BF16),
        in_specs=[vm, hbm, vm, vm, hbm, vm, vm, vm, vm, hbm, hbm, hbm, hbm],
        out_specs=vm,
        scratch_shapes=scratch,
        compiler_params=pltpu.CompilerParams(
            has_side_effects=True, vmem_limit_bytes=56 * 1024 * 1024),
    )(resid, enc, enc_bias[None], ids, dec, dec_bias[None], segs[None], gin[None], gpo[None],
      qw, kw, vw, ow)


def solution(mesh):
    return jax.shard_map(
        lambda *args: local(mesh, *args),
        mesh=mesh,
        in_specs=(
            P("dp", "tensor"),
            P(None, ("dp", "tensor")),
            P(("dp", "tensor")),
            P(),
            P("dp", "tensor"),
            P("tensor"),
            P(),
            P(),
            P(),
            P("dp", "tensor"),
            P("dp", "tensor"),
            P("dp", "tensor"),
            P("tensor", "dp"),
        ),
        out_specs=P("dp", "tensor"),
        check_vma=False,
    )
```

```python
import math

import jax
import jax.numpy as jnp
from jax import lax
from jax.experimental import pallas as pl
from jax.experimental.pallas import tpu as pltpu
from jax.sharding import PartitionSpec as P

QUERY_SCALE = 144.0 ** (-0.5)
SOFT_CAP = 50.0
EPS = 1e-06
MESH = pl.DeviceIdType.MESH
F32 = jnp.float32
BF16 = jnp.bfloat16


def dot_nt(a, b):
    return lax.dot_general(a, b, (((1,), (1,)), ((), ())), preferred_element_type=F32)


def kernel(
    NP, NT,
    resid, enc_hbm, enc_bias, ids_ref, dec_hbm, dec_bias, segs, gain_in, gain_post,
    q_hbm, k_hbm, v_hbm, o_hbm,
    out_ref,
    E, DEC, WA, WB,
    COL, X, IDT, IDP, B, VS, VR, VG, S,
    RS, RR, ZS, ZR, SPF, SP, GIN, GPO, YS, YR, QB, KV,
    CT, ST, MASK, HO, OSD, OSR, OSS, OR, NR,
    lsem, ssem, rsem, r1b, r1c, r7, r7b,
):
    T = 16 * NP
    R8 = 8 * NP
    NZ = NT // 2
    NH = NT // 2
    CH = resid.shape[1]
    D = NT * CH
    g = lax.axis_index("dp")
    s = lax.axis_index("tensor")
    zh = g // NP
    p = g % NP
    zl = s // 2
    c = s % 2
    sib = s + 1 - 2 * c

    def wrap(i, n):
        return jnp.where(i >= n, i - n, i)

    def rcopy(src, dst, k, dp, tensor, rs=None):
        return pltpu.make_async_remote_copy(
            src_ref=src, dst_ref=dst, send_sem=ssem.at[k],
            recv_sem=rsem.at[k] if rs is None else rs,
            device_id={"dp": dp, "tensor": tensor}, device_id_type=MESH)

    drains = []

    def bulk(ref, n, sem):
        d = ref.at[pl.ds(0, n)]
        pltpu.make_async_copy(d, d, sem).wait()

    def drain():
        for wait in drains:
            wait()

    def to_plane(k, src, dst, sent, rs=None):
        for j in range(1, NP):
            q = wrap(p + j, NP)
            rcopy(src(q), dst, k, zh * NP + q, s, rs).start()
        drains.append(lambda: bulk(sent, NP - 1, ssem.at[k]))

    def to_tensor(k, src, dst, sent):
        for j in range(1, NT):
            q = wrap(s + j, NT)
            rcopy(src(q), dst, k, g, q).start()
        drains.append(lambda: bulk(sent, NT - 1, ssem.at[k]))

    barrier = pltpu.get_barrier_semaphore()

    def greet(dp, tensor):
        pl.semaphore_signal(
            barrier, inc=1, device_id={"dp": dp, "tensor": tensor}, device_id_type=MESH)
    for j in range(1, NT):
        greet(g, wrap(s + j, NT))
    for j in range(NT):
        greet((1 - zh) * NP + p, j)
    for j in range(1, NP):
        greet(zh * NP + wrap(p + j, NP), s)

    loads = []
    for z in range(NZ):
        for h in range(2):
            row = pl.multiple_of((2 * z + (c if h == 0 else 1 - c)) * CH, 16)
            loads.append(pltpu.make_async_copy(
                enc_hbm.at[pl.ds(row, CH)], E.at[h, pl.ds(z * CH, CH)], lsem.at[len(loads)]))
    n_enc = len(loads)
    for a, b in (
        (dec_hbm, DEC), (q_hbm, WA.at[p, :, 0:256]), (k_hbm, WA.at[p, :, 256:384]),
        (v_hbm, WA.at[p, :, 384:512]), (o_hbm, WB.at[p]),
    ):
        loads.append(pltpu.make_async_copy(a, b, lsem.at[len(loads)]))
    for cp in loads:
        cp.start()
    me_z = zh * NZ + zl
    COL[me_z] = resid[...]

    IDT[...] = jnp.concatenate([ids_ref[:, :R8], ids_ref[:, R8:]], axis=0)
    IDP[...] = IDT[...].T
    gi, gp = gain_in[...][None], gain_post[...][None]
    for j in range(NT):
        GIN[j:j + 1, :] = gi[:, j * CH:(j + 1) * CH]
        GPO[j:j + 1, :] = gp[:, j * CH:(j + 1) * CH]

    def tok(r):
        return ((r // 8) % 2) * R8 + (r // 16) * 8 + r % 8
    segc = jnp.broadcast_to(segs[...].astype(F32)[None], (T, T)).T
    segc = jnp.concatenate(
        [segc[h * R8 + b * 8:h * R8 + b * 8 + 8] for b in range(NP) for h in range(2)], axis=0)
    tr = tok(lax.broadcasted_iota(jnp.int32, (T, T), 0))
    tc = tok(lax.broadcasted_iota(jnp.int32, (T, T), 1))
    same = segc == segc.T
    MASK[...] = jnp.where(same & (tc <= tr), 1.0, 0.0)
    pos = jnp.sum(jnp.where(same & (tc < tr), 1.0, 0.0), axis=1, keepdims=True)
    lane = lax.broadcasted_iota(jnp.int32, (1, 128), 1)
    inverse = jnp.exp((lane % 64).astype(F32) * (-2.0 * math.log(10000.0) / 128))
    ang = pos * inverse
    CT[...] = jnp.cos(ang)
    ST[...] = jnp.where(lane < 64, -1.0, 1.0) * jnp.sin(ang)

    pl.semaphore_wait(barrier, 2 * NT - 1 + NP - 1)
    for j in range(1, 2 * NZ):
        z = wrap(me_z + j, 2 * NZ)
        far = jnp.where(z >= NZ, 1, 0)
        rcopy(resid, COL.at[me_z], 0, far * NP + p, (z - far * NZ) * 2 + c).start()
    drains.append(lambda: bulk(COL, 2 * NZ - 1, ssem.at[0]))

    @pl.loop(0, NP)
    def _(b):
        lo = (IDP[pl.ds(pl.multiple_of(b * 8, 8), 8), :] & 255).astype(F32).T
        cols = lax.broadcasted_iota(jnp.int32, (128, 256), 1).astype(F32)
        for i in range(8):
            B[b, pl.ds(i * 128, 128), :] = jnp.where(lo[:, i:i + 1] == cols, 1.0, 0.0).astype(BF16)

    bulk(COL, 2 * NZ - 1, rsem.at[0])
    halves = []
    for h in range(2):
        halves.append(jnp.concatenate(
            [COL[h * NZ + z].astype(F32) for z in range(NZ)], axis=1))
    X[0, p] = jnp.concatenate(halves, axis=0).astype(BF16)
    to_plane(1, lambda q: X.at[0, p], X.at[0, p], X.at[0], r1b.at[p])
    rcopy(X.at[0, p], X.at[1, p], 2, g, sib, r1c.at[p]).start()
    drains.append(lambda: bulk(X.at[0], NP, ssem.at[2]))
    for j in range(1, NP):
        q = wrap(p + NP - j, NP)
        pltpu.make_async_copy(X.at[0, q], X.at[0, q], r1b.at[q]).wait()
        rcopy(X.at[0, q], X.at[1, q], 2, g, sib, r1c.at[q]).start()

    for cp in loads[n_enc + 1:]:
        cp.wait()
    to_plane(8, lambda q: WA.at[p], WA.at[p], WA)
    to_plane(9, lambda q: WB.at[p], WB.at[p], WB)

    for cp in loads[:n_enc]:
        cp.wait()
    pre = jnp.dot(X[0].reshape(T, NZ * CH), E[0], preferred_element_type=F32)
    for q in range(NP):
        pltpu.make_async_copy(X.at[1, q], X.at[1, q], r1c.at[q]).wait()
    pre = pre + jnp.dot(X[1].reshape(T, NZ * CH), E[1], preferred_element_type=F32)
    act = jnp.maximum(pre + enc_bias[...][None], 0.0).astype(BF16).astype(F32)

    act = act.reshape(NP, 2, 8, 256)
    a0 = act[:, 0].reshape(R8, 256)
    a1 = act[:, 1].reshape(R8, 256)
    rel = IDP[...] - (g * NT + s) * 256
    low = rel & 127
    left = lax.broadcasted_iota(jnp.int32, (R8, 128), 1) < 64

    def pick(h):
        return jnp.where(
            left,
            jnp.take_along_axis(a0[:, h * 128:(h + 1) * 128], low, axis=1),
            jnp.take_along_axis(a1[:, h * 128:(h + 1) * 128], low, axis=1))
    val = jnp.where(rel >= 128, pick(1), pick(0))
    val = jnp.where((rel >= 0) & (rel < 256), val, 0.0)
    VS[...] = val.reshape(NT, 8, 128)
    VR[s] = VS[s]
    to_tensor(3, lambda q: VS.at[q], VR.at[s], VS)
    bulk(VR, NT - 1, rsem.at[3])
    VG[s] = jnp.sum(VR[...], axis=0)
    to_tensor(4, lambda q: VG.at[s], VG.at[s], VG)
    bulk(VG, NT - 1, rsem.at[4])

    sub = lax.broadcasted_iota(jnp.int32, (8, 128), 0)
    lft = lax.broadcasted_iota(jnp.int32, (8, 128), 1) < 64
    @pl.loop(0, NP)
    def _(b):
        relb = IDP[pl.ds(pl.multiple_of(b * 8, 8), 8), :] - g * (NT * 256)
        vb = VG[b]
        hi = jnp.where(relb < 0, -1, relb >> 8)
        v0 = jnp.where(lft, vb, 0.0)
        v1 = vb - v0
        rows = []
        for h in range(NT):
            for vz in (v0, v1):
                d = jnp.where(hi == h, vz, 0.0)
                rows.append(jnp.concatenate([jnp.where(sub == i, d, 0.0) for i in range(8)], axis=1))
        lhs = jnp.concatenate(rows, axis=0).astype(BF16)
        sel = jnp.dot(lhs, B[b], preferred_element_type=F32).astype(BF16)
        S[:, pl.ds(pl.multiple_of(b * 16, 16), 16), :] = sel.reshape(NT, 16, 256)
    loads[n_enc].wait()
    rec = dot_nt(S[0], DEC[:, 0:256])
    for h in range(1, NT):
        rec = rec + dot_nt(S[h], DEC[:, h * 256:(h + 1) * 256])
    RS[...] = rec.reshape(NP, 16, CH)
    RR[p] = RS[p]
    to_plane(5, lambda q: RS.at[q], RR.at[p], RS)
    bulk(RR, NP - 1, rsem.at[5])
    ZS[...] = jnp.sum(RR[...], axis=0)
    zp = (1 - zh) * NP + p
    zc = rcopy(ZS, ZR, 6, zp, s)
    zc.start()
    drains.append(zc.wait_send)
    zc.wait_recv()
    spl = (ZS[...] + ZR[...] + dec_bias[...][None]).astype(BF16)
    SPF[...] = spl.astype(F32).reshape(2, 8, CH)
    SP[s] = spl

    rcopy(SP.at[s], SP.at[s], 10, g, sib, r7b.at[zl]).start()
    for j in range(1, NZ):
        rcopy(SP.at[s], SP.at[s], 7, g, 2 * wrap(zl + j, NZ) + c, r7.at[zl]).start()
    if NZ > 1:
        drains.append(lambda: bulk(SP, NZ - 1, ssem.at[7]))
    drains.append(lambda: bulk(SP, NZ, ssem.at[10]))
    for j in range(1, NZ):
        z = wrap(zl + NZ - j, NZ)
        there = SP.at[2 * z + c]
        pltpu.make_async_copy(there, there, r7.at[z]).wait()
        rcopy(there, there, 10, g, sib, r7b.at[z]).start()
    for z in range(NZ):
        pltpu.make_async_copy(SP.at[0], SP.at[0], r7b.at[z]).wait()

    ss = jnp.zeros((16, 1), F32)
    for j in range(NT):
        xj = SP[j].astype(F32)
        ss = ss + jnp.sum(xj * xj, axis=1, keepdims=True)
    rn = lax.rsqrt(ss / D + EPS)
    normed = []
    for j in range(NH):
        cj = zh * NH + j
        normed.append(SP[cj].astype(F32) * rn * GIN[pl.ds(cj, 1), :])
    normed = jnp.concatenate(normed, axis=1).astype(BF16)
    bulk(WA, NP - 1, rsem.at[8])
    YS[...] = jnp.dot(normed, WA[...].reshape(NH * CH, 512), preferred_element_type=F32)
    yc = rcopy(YS, YR, 11, zp, s)
    yc.start()
    drains.append(yc.wait_send)
    yc.wait_recv()
    y = YS[...] + YR[...]
    mine = pl.ds(pl.multiple_of(p * 16, 16), 16)
    cosine, sine = CT[mine, :], ST[mine, :]

    def rot(x):
        return x * cosine + pltpu.roll(x, 64, 1) * sine
    KV[p] = jnp.concatenate([rot(y[:, 256:384]), y[:, 384:512]], axis=1).astype(BF16)
    to_plane(12, lambda q: KV.at[p], KV.at[p], KV)
    QB[...] = jnp.concatenate(
        [rot(y[:, 0:128]) * QUERY_SCALE, rot(y[:, 128:256]) * QUERY_SCALE], axis=1).astype(BF16)
    bulk(KV, NP - 1, rsem.at[12])

    kk = KV[:, :, 0:128].reshape(T, 128)
    vv = KV[:, :, 128:256].reshape(T, 128)
    allowed = MASK[mine, :] > 0.0
    for h in range(2):
        sc = dot_nt(QB[:, h * 128:(h + 1) * 128], kk)
        w = jnp.where(allowed, jnp.exp(SOFT_CAP * jnp.tanh(sc / SOFT_CAP)), 0.0)
        tot = jnp.sum(w, axis=1, keepdims=True)
        mixed = jnp.dot(w.astype(BF16), vv, preferred_element_type=F32)
        HO[:, h * 128:(h + 1) * 128] = (mixed / tot).astype(BF16)
    bulk(WB, NP - 1, rsem.at[9])
    for j in range(NH):
        o = dot_nt(HO[...], WB[pl.ds(2 * j, 2)].reshape(CH, 256))
        OSD[0, j] = o[:8]
        OSD[1, j] = o[8:]

    oc = rcopy(OSD.at[1 - c], OSR, 13, g, sib)
    oc.start()
    drains.append(oc.wait_send)
    oc.wait_recv()
    OSS[...] = OSD[c] + OSR[...]
    own = (c == zh) & (s // NH == zh)
    for j in range(NH):
        here = (c == zh) & (zh * NH + j == s)

        @pl.when(here)
        def _():
            OR[zl] = OSS[j]

        @pl.when(jnp.logical_not(here))
        def _():
            rcopy(OSS.at[j], OR.at[zl], 14, c * NP + p, zh * NH + j).start()

    def bulk_own(ref, sem):
        @pl.when(own)
        def _():
            if NZ > 1:
                bulk(ref, NZ - 1, sem)

        @pl.when(jnp.logical_not(own))
        def _():
            bulk(ref, NZ, sem)
    drains.append(lambda: bulk_own(OSS, ssem.at[14]))
    bulk_own(OR, rsem.at[14])
    att = jnp.sum(OR[...], axis=0)
    NR[s] = jnp.broadcast_to(jnp.sum(att * att, axis=1, keepdims=True), (8, 128))
    to_tensor(15, lambda q: NR.at[s], NR.at[s], NR)
    bulk(NR, NT - 1, rsem.at[15])
    tot = jnp.sum(NR[...], axis=0)[:, 0:1]
    post = att * lax.rsqrt(tot / D + EPS) * GPO[pl.ds(s, 1), :]
    out_ref[...] = (SPF[zh] + post).astype(BF16)
    drain()


def local(mesh, resid, enc, enc_bias, ids, dec, dec_bias, segs, gin, gpo, qw, kw, vw, ow):
    NT = mesh.shape["tensor"]
    NP = mesh.shape["dp"] // 2
    assert NT == NP
    T, CH, NZ = 16 * NP, resid.shape[1], NT // 2
    HC = CH // 2
    V = pltpu.VMEM
    scratch = [
        V((2, NZ * CH, 256), BF16), V(dec.shape[::-1], BF16), V((NP, HC, 512), BF16),
        V((NP, HC, 256), BF16),
        V((2 * NZ, 8, CH), BF16), V((2, NP, 16, NZ * CH), BF16), V((128, 8 * NP), jnp.int32),
        V((8 * NP, 128), jnp.int32), V((NP, 1024, 256), BF16),
        V((NT, 8, 128), F32), V((NT, 8, 128), F32), V((NT, 8, 128), F32), V((NT, T, 256), BF16),
        V((NP, 16, CH), F32), V((NP, 16, CH), F32), V((16, CH), F32), V((16, CH), F32),
        V((2, 8, CH), F32), V((NT, 16, CH), BF16), V((NT, CH), F32), V((NT, CH), F32),
        V((16, 512), F32), V((16, 512), F32), V((16, 256), BF16), V((NP, 16, 256), BF16),
        V((T, 128), F32), V((T, 128), F32), V((T, T), F32), V((16, 256), BF16),
        V((2, NZ, 8, CH), F32), V((NZ, 8, CH), F32), V((NZ, 8, CH), F32), V((NZ, 8, CH), F32),
        V((NT, 8, 128), F32),
        pltpu.SemaphoreType.DMA((2 * NZ + 5,)), pltpu.SemaphoreType.DMA((16,)),
        pltpu.SemaphoreType.DMA((16,)), pltpu.SemaphoreType.DMA((NP,)), pltpu.SemaphoreType.DMA((NP,)),
        pltpu.SemaphoreType.DMA((NZ,)), pltpu.SemaphoreType.DMA((NZ,)),
    ]
    vm = pl.BlockSpec(memory_space=V)
    hbm = pl.BlockSpec(memory_space=pl.ANY)
    return pl.pallas_call(
        lambda *refs: kernel(NP, NT, *refs),
        out_shape=jax.ShapeDtypeStruct((8, CH), BF16),
        in_specs=[vm, hbm, vm, vm, hbm, vm, vm, vm, vm, hbm, hbm, hbm, hbm],
        out_specs=vm,
        scratch_shapes=scratch,
        compiler_params=pltpu.CompilerParams(
            collective_id=0, has_side_effects=True, vmem_limit_bytes=56 * 1024 * 1024),
    )(resid, enc, enc_bias, ids.T, dec.T, dec_bias, segs, gin, gpo, qw, kw, vw, ow.T)


def solution(mesh):
    return jax.shard_map(
        lambda *args: local(mesh, *args),
        mesh=mesh,
        in_specs=(
            P("dp", "tensor"),
            P(None, ("dp", "tensor")),
            P(("dp", "tensor")),
            P(),
            P("dp", "tensor"),
            P("tensor"),
            P(),
            P(),
            P(),
            P("dp", "tensor"),
            P("dp", "tensor"),
            P("dp", "tensor"),
            P("tensor", "dp"),
        ),
        out_specs=P("dp", "tensor"),
        check_vma=False,
    )
```

```python
import math

import jax
import jax.numpy as jnp
from jax import lax
from jax.experimental import pallas as pl
from jax.experimental.pallas import tpu as pltpu
from jax.sharding import PartitionSpec as P

QUERY_SCALE = 144.0 ** (-0.5)
SOFT_CAP = 50.0
EPS = 1e-06
MESH = pl.DeviceIdType.MESH
F32 = jnp.float32
BF16 = jnp.bfloat16


def dot_nt(a, b):
    return lax.dot_general(a, b, (((1,), (1,)), ((), ())), preferred_element_type=F32)


def kernel(
    NP, NT, NX, NY,
    resid, enc_hbm, enc_bias, ids_ref, dec_hbm, dec_bias, segs, gain_in, gain_post,
    q_hbm, k_hbm, v_hbm, o_hbm,
    out_ref,
    E, DEC, WQ, WK, WB,
    COL, X, IDT, IDP, B, VS, VR, VG, S,
    RS, RR, ZS, ZR, SPF, SP, GIN, GPO, YKS, YKR, YQS, YQR, QB, KV,
    SEGC, HO, OSD, OSR, OSS, OR, NR,
    lsem, ssem, rsem, r2x, r2y, r7, r7b,
):
    T = 16 * NP
    R8 = 8 * NP
    NZ = NT // 2
    NH = NT // 2
    CH = resid.shape[1]
    D = NT * CH
    g = lax.axis_index("dp")
    s = lax.axis_index("tensor")
    zh = g // NP
    p = g % NP
    zl = s // 2
    c = s % 2
    x = p % NX
    y = p // NX
    sib = s + 1 - 2 * c

    def wrap(i, n):
        return jnp.where(i >= n, i - n, i)

    def rcopy(src, dst, k, dp, tensor, rs=None):
        return pltpu.make_async_remote_copy(
            src_ref=src, dst_ref=dst, send_sem=ssem.at[k],
            recv_sem=rsem.at[k] if rs is None else rs,
            device_id={"dp": dp, "tensor": tensor}, device_id_type=MESH)

    drains = []

    def bulk(ref, n, sem):
        d = ref.at[pl.ds(0, n)]
        pltpu.make_async_copy(d, d, sem).wait()

    def land(ref, sem):
        pltpu.make_async_copy(ref, ref, sem).wait()

    def drain():
        for wait in drains:
            wait()

    def to_plane(k, src, dst, sent, rs=None):
        for j in range(1, NP):
            q = wrap(p + j, NP)
            rcopy(src(q), dst, k, zh * NP + q, s, rs).start()
        drains.append(lambda: bulk(sent, NP - 1, ssem.at[k]))

    def to_x(k, src, dst, many, rs=None):
        for j in range(1, NX):
            rcopy(src, dst, k, zh * NP + y * NX + wrap(x + j, NX), s, rs).start()
        drains.append(lambda: land(many, ssem.at[k]))

    def to_y(k, src, dst, many, rs=None):
        for j in range(1, NY):
            rcopy(src, dst, k, zh * NP + wrap(y + j, NY) * NX + x, s, rs).start()
        drains.append(lambda: land(many, ssem.at[k]))

    def to_tensor(k, src, dst, sent):
        for j in range(1, NT):
            q = wrap(s + j, NT)
            rcopy(src(q), dst, k, g, q).start()
        drains.append(lambda: bulk(sent, NT - 1, ssem.at[k]))

    barrier = pltpu.get_barrier_semaphore()

    def greet(dp, tensor):
        pl.semaphore_signal(
            barrier, inc=1, device_id={"dp": dp, "tensor": tensor}, device_id_type=MESH)
    for j in range(1, NT):
        greet(g, wrap(s + j, NT))
    for j in range(NT):
        greet((1 - zh) * NP + p, j)
    for j in range(1, NP):
        greet(zh * NP + wrap(p + j, NP), s)

    loads = []
    for z in range(NZ):
        for h in range(2):
            row = pl.multiple_of((2 * z + (c if h == 0 else 1 - c)) * CH, 16)
            loads.append(pltpu.make_async_copy(
                enc_hbm.at[pl.ds(row, CH)], E.at[h, pl.ds(z * CH, CH)], lsem.at[len(loads)]))
    n_enc = len(loads)
    for a, b in (
        (dec_hbm, DEC), (q_hbm, WQ.at[y, x]), (k_hbm, WK.at[y, x, :, 0:128]),
        (v_hbm, WK.at[y, x, :, 128:256]), (o_hbm, WB.at[y, x]),
    ):
        loads.append(pltpu.make_async_copy(a, b, lsem.at[len(loads)]))
    for cp in loads:
        cp.start()
    me_z = zh * NZ + zl
    COL[me_z] = resid[...]

    IDT[...] = jnp.concatenate([ids_ref[:, :R8], ids_ref[:, R8:]], axis=0)
    IDP[...] = IDT[...].T
    gi, gp = gain_in[...][None], gain_post[...][None]
    for j in range(NT):
        GIN[j:j + 1, :] = gi[:, j * CH:(j + 1) * CH]
        GPO[j:j + 1, :] = gp[:, j * CH:(j + 1) * CH]

    segc = jnp.broadcast_to(segs[...].astype(F32)[None], (128, T)).T
    SEGC[...] = jnp.concatenate(
        [segc[h * R8 + b * 8:h * R8 + b * 8 + 8] for b in range(NP) for h in range(2)], axis=0)
    mine = pl.ds(pl.multiple_of(p * 16, 16), 16)
    same = SEGC[mine, :][:, 0:1] == SEGC[...].T[0:1, :]
    row = lax.broadcasted_iota(jnp.int32, (16, 1), 0)
    col = lax.broadcasted_iota(jnp.int32, (1, T), 1)
    tr = (row >> 3) * R8 + p * 8 + (row & 7)
    tc = ((col >> 3) & 1) * R8 + (col >> 4) * 8 + (col & 7)
    allowed = same & (tc <= tr)
    pos = jnp.sum(jnp.where(same & (tc < tr), 1.0, 0.0), axis=1, keepdims=True)
    lane = lax.broadcasted_iota(jnp.int32, (1, 128), 1)
    inverse = jnp.exp((lane & 63).astype(F32) * (-2.0 * math.log(10000.0) / 128))
    ang = pos * inverse
    cosine = jnp.cos(ang)
    sine = jnp.where(lane < 64, -1.0, 1.0) * jnp.sin(ang)

    pl.semaphore_wait(barrier, 2 * NT - 1 + NP - 1)
    for j in range(1, 2 * NZ):
        z = wrap(me_z + j, 2 * NZ)
        far = jnp.where(z >= NZ, 1, 0)
        rcopy(resid, COL.at[me_z], 0, far * NP + p, (z - far * NZ) * 2 + c).start()
    drains.append(lambda: bulk(COL, 2 * NZ - 1, ssem.at[0]))

    @pl.loop(0, NP)
    def _(b):
        lo = (IDP[pl.ds(pl.multiple_of(b * 8, 8), 8), :] & 255).astype(F32).T
        cols = lax.broadcasted_iota(jnp.int32, (128, 256), 1).astype(F32)
        for i in range(8):
            B[b, pl.ds(i * 128, 128), :] = jnp.where(lo[:, i:i + 1] == cols, 1.0, 0.0).astype(BF16)

    bulk(COL, 2 * NZ - 1, rsem.at[0])
    halves = []
    for h in range(2):
        halves.append(jnp.concatenate(
            [COL[h * NZ + z].astype(F32) for z in range(NZ)], axis=1))
    X[0, y, x] = jnp.concatenate(halves, axis=0).astype(BF16)
    F2 = NZ * CH
    A, Bh = pl.ds(0, F2 // 2), pl.ds(F2 // 2, F2 // 2)

    def on(*where):
        rcopy(X.at[(0,) + where], X.at[(1,) + where], 2, g, sib, rsem.at[2]).start()
    own_a, own_b = X.at[0, y, x, :, A], X.at[0, y, x, :, Bh]
    row_a, col_b = X.at[0, y, :, :, A], X.at[0, :, x, :, Bh]
    own_as, own_bs = X.at[0, y, pl.ds(0, NX - 1), :, A], X.at[0, pl.ds(0, NY - 1), x, :, Bh]
    row_as, col_bs = X.at[0, pl.ds(0, NY - 1), :, :, A], X.at[0, :, pl.ds(0, NX - 1), :, Bh]
    to_x(1, own_a, own_a, own_as)
    to_y(17, own_b, own_b, own_bs)
    land(own_as, rsem.at[1])
    to_y(18, row_a, row_a, row_as, r2y.at[y])
    land(own_bs, rsem.at[17])
    to_x(19, col_b, col_b, col_bs, r2x.at[x])
    on(y, slice(None), slice(None), A)
    on(slice(None), x, slice(None), Bh)

    for cp in loads[n_enc + 1:]:
        cp.wait()
    lo, hi = pl.ds(0, 80), pl.ds(80, 64)
    nx, ny = pl.ds(0, NX - 1), pl.ds(0, NY - 1)
    own_q, own_k, own_ba, own_bb = WQ.at[y, x], WK.at[y, x], WB.at[y, x, lo], WB.at[y, x, hi]
    own_qs, own_ks, own_bas, own_bbs = WQ.at[y, nx], WK.at[ny, x], WB.at[y, nx, lo], WB.at[ny, x, hi]
    row_q, col_k, row_b, col_bb = WQ.at[y], WK.at[:, x], WB.at[y, :, lo], WB.at[:, x, hi]
    row_qs, col_ks, row_bs, col_bbs = WQ.at[ny], WK.at[:, nx], WB.at[ny, :, lo], WB.at[:, nx, hi]
    to_x(8, own_q, own_q, own_qs)
    to_y(9, own_k, own_k, own_ks)
    to_x(16, own_ba, own_ba, own_bas)
    to_y(20, own_bb, own_bb, own_bbs)
    for j in range(1, max(NX, NY)):
        if j < NY:
            yy = wrap(y + NY - j, NY)
            land(row_a, r2y.at[yy])
            on(yy, slice(None), slice(None), A)
        if j < NX:
            xx = wrap(x + NX - j, NX)
            land(col_b, r2x.at[xx])
            on(slice(None), xx, slice(None), Bh)
    drains.append(lambda: land(X.at[0], ssem.at[2]))
    land(own_qs, rsem.at[8])
    to_y(21, row_q, row_q, row_qs)
    land(own_ks, rsem.at[9])
    to_x(22, col_k, col_k, col_ks)
    land(own_bas, rsem.at[16])
    to_y(23, row_b, row_b, row_bs)
    land(own_bbs, rsem.at[20])
    to_x(24, col_bb, col_bb, col_bbs)

    for cp in loads[:n_enc]:
        cp.wait()
    pre = jnp.dot(X[0].reshape(T, F2), E[0], preferred_element_type=F32)
    land(X.at[1], rsem.at[2])
    pre = pre + jnp.dot(X[1].reshape(T, F2), E[1], preferred_element_type=F32)
    act = jnp.maximum(pre + enc_bias[...][None], 0.0).astype(BF16).astype(F32)

    act = act.reshape(NP, 2, 8, 256)
    a0 = act[:, 0].reshape(R8, 256)
    a1 = act[:, 1].reshape(R8, 256)
    rel = IDP[...] - (g * NT + s) * 256
    low = rel & 127
    left = lax.broadcasted_iota(jnp.int32, (R8, 128), 1) < 64

    def pick(h):
        return jnp.where(
            left,
            jnp.take_along_axis(a0[:, h * 128:(h + 1) * 128], low, axis=1),
            jnp.take_along_axis(a1[:, h * 128:(h + 1) * 128], low, axis=1))
    val = jnp.where(rel >= 128, pick(1), pick(0))
    val = jnp.where((rel >= 0) & (rel < 256), val, 0.0)
    VS[...] = val.reshape(NT, 8, 128).astype(BF16)
    VR[s] = VS[s]
    to_tensor(3, lambda q: VS.at[q], VR.at[s], VS)
    bulk(VR, NT - 1, rsem.at[3])
    VG[s] = jnp.sum(VR[...].astype(F32), axis=0).astype(BF16)
    to_tensor(4, lambda q: VG.at[s], VG.at[s], VG)
    bulk(VG, NT - 1, rsem.at[4])

    sub = lax.broadcasted_iota(jnp.int32, (8, 128), 0)
    lft = lax.broadcasted_iota(jnp.int32, (8, 128), 1) < 64
    @pl.loop(0, NP)
    def _(b):
        relb = IDP[pl.ds(pl.multiple_of(b * 8, 8), 8), :] - g * (NT * 256)
        vb = VG[b].astype(F32)
        hi = jnp.where(relb < 0, -1, relb >> 8)
        v0 = jnp.where(lft, vb, 0.0)
        v1 = vb - v0
        rows = []
        for h in range(NT):
            for vz in (v0, v1):
                d = jnp.where(hi == h, vz, 0.0)
                rows.append(jnp.concatenate([jnp.where(sub == i, d, 0.0) for i in range(8)], axis=1))
        lhs = jnp.concatenate(rows, axis=0).astype(BF16)
        sel = jnp.dot(lhs, B[b], preferred_element_type=F32).astype(BF16)
        S[:, pl.ds(pl.multiple_of(b * 16, 16), 16), :] = sel.reshape(NT, 16, 256)
    loads[n_enc].wait()
    rec = dot_nt(S[0], DEC[:, 0:256])
    for h in range(1, NT):
        rec = rec + dot_nt(S[h], DEC[:, h * 256:(h + 1) * 256])
    RS[...] = rec.reshape(NP, 16, CH)
    RR[p] = RS[p]
    to_plane(5, lambda q: RS.at[q], RR.at[p], RS)
    bulk(RR, NP - 1, rsem.at[5])
    ZS[...] = jnp.sum(RR[...], axis=0)
    zp = (1 - zh) * NP + p
    zc = rcopy(ZS, ZR, 6, zp, s)
    zc.start()
    drains.append(zc.wait_send)
    zc.wait_recv()
    spl = (ZS[...] + ZR[...] + dec_bias[...][None]).astype(BF16)
    SPF[...] = spl.astype(F32).reshape(2, 8, CH)
    SP[s] = spl

    rcopy(SP.at[s], SP.at[s], 10, g, sib, r7b.at[zl]).start()
    for j in range(1, NZ):
        rcopy(SP.at[s], SP.at[s], 7, g, 2 * wrap(zl + j, NZ) + c, r7.at[zl]).start()
    if NZ > 1:
        drains.append(lambda: bulk(SP, NZ - 1, ssem.at[7]))
    drains.append(lambda: bulk(SP, NZ, ssem.at[10]))
    for j in range(1, NZ):
        z = wrap(zl + NZ - j, NZ)
        there = SP.at[2 * z + c]
        pltpu.make_async_copy(there, there, r7.at[z]).wait()
        rcopy(there, there, 10, g, sib, r7b.at[z]).start()
    for z in range(NZ):
        pltpu.make_async_copy(SP.at[0], SP.at[0], r7b.at[z]).wait()

    ss = jnp.zeros((16, 1), F32)
    for j in range(NT):
        xj = SP[j].astype(F32)
        ss = ss + jnp.sum(xj * xj, axis=1, keepdims=True)
    rn = lax.rsqrt(ss / D + EPS)
    normed = []
    for j in range(NH):
        cj = zh * NH + j
        normed.append(SP[cj].astype(F32) * rn * GIN[pl.ds(cj, 1), :])
    normed = jnp.concatenate(normed, axis=1).astype(BF16)
    land(col_ks, rsem.at[22])
    YKS[...] = jnp.dot(normed, WK[...].reshape(NH * CH, 256), preferred_element_type=F32)
    kc = rcopy(YKS, YKR, 11, zp, s)
    kc.start()
    drains.append(kc.wait_send)
    land(row_qs, rsem.at[21])
    YQS[...] = jnp.dot(normed, WQ[...].reshape(NH * CH, 256), preferred_element_type=F32)
    qc = rcopy(YQS, YQR, 25, zp, s)
    qc.start()
    drains.append(qc.wait_send)

    def rot(v):
        return v * cosine + pltpu.roll(v, 64, 1) * sine
    kc.wait_recv()
    kv = YKS[...] + YKR[...]
    KV[p] = jnp.concatenate([rot(kv[:, 0:128]), kv[:, 128:256]], axis=1).astype(BF16)
    to_plane(12, lambda q: KV.at[p], KV.at[p], KV)
    qc.wait_recv()
    qs = YQS[...] + YQR[...]
    QB[...] = jnp.concatenate(
        [rot(qs[:, 0:128]) * QUERY_SCALE, rot(qs[:, 128:256]) * QUERY_SCALE], axis=1).astype(BF16)
    bulk(KV, NP - 1, rsem.at[12])

    kk = KV[:, :, 0:128].reshape(T, 128)
    vv = KV[:, :, 128:256].reshape(T, 128)
    for h in range(2):
        sc = dot_nt(QB[:, h * 128:(h + 1) * 128], kk)
        w = jnp.where(allowed, jnp.exp(SOFT_CAP * jnp.tanh(sc / SOFT_CAP)), 0.0)
        tot = jnp.sum(w, axis=1, keepdims=True)
        mixed = jnp.dot(w.astype(BF16), vv, preferred_element_type=F32)
        HO[:, h * 128:(h + 1) * 128] = (mixed / tot).astype(BF16)
    land(row_bs, rsem.at[23])
    land(col_bbs, rsem.at[24])
    wb = WB[...].reshape(NH * CH, 256)
    for j in range(NH):
        o = dot_nt(HO[...], wb[j * CH:(j + 1) * CH])
        OSD[0, j] = o[:8]
        OSD[1, j] = o[8:]

    oc = rcopy(OSD.at[1 - c], OSR, 13, g, sib)
    oc.start()
    drains.append(oc.wait_send)
    oc.wait_recv()
    OSS[...] = OSD[c] + OSR[...]
    own = (c == zh) & (s // NH == zh)
    for j in range(NH):
        here = (c == zh) & (zh * NH + j == s)

        @pl.when(here)
        def _():
            OR[zl] = OSS[j]

        @pl.when(jnp.logical_not(here))
        def _():
            rcopy(OSS.at[j], OR.at[zl], 14, c * NP + p, zh * NH + j).start()

    def bulk_own(ref, sem):
        @pl.when(own)
        def _():
            if NZ > 1:
                bulk(ref, NZ - 1, sem)

        @pl.when(jnp.logical_not(own))
        def _():
            bulk(ref, NZ, sem)
    drains.append(lambda: bulk_own(OSS, ssem.at[14]))
    bulk_own(OR, rsem.at[14])
    att = jnp.sum(OR[...], axis=0)
    diag = lax.broadcasted_iota(jnp.int32, (8, 128), 0) == lax.broadcasted_iota(jnp.int32, (8, 128), 1)
    NR[s] = jnp.sum(jnp.where(diag, jnp.sum(att * att, axis=1, keepdims=True), 0.0), axis=0, keepdims=True)
    to_tensor(15, lambda q: NR.at[s], NR.at[s], NR)
    bulk(NR, NT - 1, rsem.at[15])
    tot = jnp.sum(jnp.where(diag, jnp.sum(NR[...], axis=0), 0.0), axis=1, keepdims=True)
    post = att * lax.rsqrt(tot / D + EPS) * GPO[pl.ds(s, 1), :]
    out_ref[...] = (SPF[zh] + post).astype(BF16)
    drain()


def local(mesh, resid, enc, enc_bias, ids, dec, dec_bias, segs, gin, gpo, qw, kw, vw, ow):
    NT = mesh.shape["tensor"]
    NP = mesh.shape["dp"] // 2
    assert NT == NP
    T, CH, NZ = 16 * NP, resid.shape[1], NT // 2
    HC = CH // 2
    NX = 1 << (NP.bit_length() // 2)
    NY = NP // NX
    V = pltpu.VMEM
    scratch = [
        V((2, NZ * CH, 256), BF16), V(dec.shape[::-1], BF16), V((NY, NX, HC, 256), BF16),
        V((NY, NX, HC, 256), BF16), V((NY, NX, HC, 256), BF16),
        V((2 * NZ, 8, CH), BF16), V((2, NY, NX, 16, NZ * CH), BF16), V((128, 8 * NP), jnp.int32),
        V((8 * NP, 128), jnp.int32), V((NP, 1024, 256), BF16),
        V((NT, 8, 128), BF16), V((NT, 8, 128), BF16), V((NT, 8, 128), BF16), V((NT, T, 256), BF16),
        V((NP, 16, CH), F32), V((NP, 16, CH), F32), V((16, CH), F32), V((16, CH), F32),
        V((2, 8, CH), F32), V((NT, 16, CH), BF16), V((NT, CH), F32), V((NT, CH), F32),
        V((16, 256), F32), V((16, 256), F32), V((16, 256), F32), V((16, 256), F32), V((16, 256), BF16), V((NP, 16, 256), BF16),
        V((T, 128), F32), V((16, 256), BF16),
        V((2, NZ, 8, CH), F32), V((NZ, 8, CH), F32), V((NZ, 8, CH), F32), V((NZ, 8, CH), F32),
        V((NT, 1, 128), F32),
        pltpu.SemaphoreType.DMA((2 * NZ + 5,)), pltpu.SemaphoreType.DMA((26,)),
        pltpu.SemaphoreType.DMA((26,)), pltpu.SemaphoreType.DMA((NX,)), pltpu.SemaphoreType.DMA((NY,)),
        pltpu.SemaphoreType.DMA((NZ,)), pltpu.SemaphoreType.DMA((NZ,)),
    ]
    vm = pl.BlockSpec(memory_space=V)
    hbm = pl.BlockSpec(memory_space=pl.ANY)
    return pl.pallas_call(
        lambda *refs: kernel(NP, NT, NX, NY, *refs),
        out_shape=jax.ShapeDtypeStruct((8, CH), BF16),
        in_specs=[vm, hbm, vm, vm, hbm, vm, vm, vm, vm, hbm, hbm, hbm, hbm],
        out_specs=vm,
        scratch_shapes=scratch,
        compiler_params=pltpu.CompilerParams(
            collective_id=0, has_side_effects=True, vmem_limit_bytes=56 * 1024 * 1024),
    )(resid, enc, enc_bias, ids.T, dec.T, dec_bias, segs, gin, gpo, qw, kw, vw, ow.T)


def solution(mesh):
    return jax.shard_map(
        lambda *args: local(mesh, *args),
        mesh=mesh,
        in_specs=(
            P("dp", "tensor"),
            P(None, ("dp", "tensor")),
            P(("dp", "tensor")),
            P(),
            P("dp", "tensor"),
            P("tensor"),
            P(),
            P(),
            P(),
            P("dp", "tensor"),
            P("dp", "tensor"),
            P("dp", "tensor"),
            P("tensor", "dp"),
        ),
        out_specs=P("dp", "tensor"),
        check_vma=False,
    )
```

```python
import math

import jax
import jax.numpy as jnp
from jax import lax
from jax.experimental import pallas as pl
from jax.experimental.pallas import tpu as pltpu
from jax.sharding import PartitionSpec as P

QUERY_SCALE = 144.0 ** (-0.5)
SOFT_CAP = 50.0
EPS = 1e-06
MESH = pl.DeviceIdType.MESH
F32 = jnp.float32
BF16 = jnp.bfloat16


def dot_nt(a, b):
    return lax.dot_general(a, b, (((1,), (1,)), ((), ())), preferred_element_type=F32)


def kernel(
    NP, NT, NX, NY,
    resid, enc_hbm, enc_bias, ids_ref, dec_hbm, dec_bias, segs, gain_in, gain_post,
    q_hbm, k_hbm, v_hbm, o_hbm,
    out_ref,
    E, DEC, WQ, WK, WB,
    COL, X, IDT, IDP, B, VS, VR, VG, S,
    RS, RR, ZS, ZR, SPF, SP, GIN, GPO, YKS, YKR, YQS, YQR, QB, KV,
    SEGC, HO, OSD, OSR, OSS, OR, NR,
    lsem, ssem, rsem, r2x, r2y, r7, r7b,
):
    T = 16 * NP
    R8 = 8 * NP
    NZ = NT // 2
    NH = NT // 2
    CH = resid.shape[1]
    D = NT * CH
    g = lax.axis_index("dp")
    s = lax.axis_index("tensor")
    zh = g // NP
    p = g % NP
    zl = s // 2
    c = s % 2
    x = p % NX
    y = p // NX
    sib = s + 1 - 2 * c

    def wrap(i, n):
        return jnp.where(i >= n, i - n, i)

    def rcopy(src, dst, k, dp, tensor, rs=None):
        return pltpu.make_async_remote_copy(
            src_ref=src, dst_ref=dst, send_sem=ssem.at[k],
            recv_sem=rsem.at[k] if rs is None else rs,
            device_id={"dp": dp, "tensor": tensor}, device_id_type=MESH)

    drains = []

    def bulk(ref, n, sem):
        d = ref.at[pl.ds(0, n)]
        pltpu.make_async_copy(d, d, sem).wait()

    def land(ref, sem):
        pltpu.make_async_copy(ref, ref, sem).wait()

    def drain():
        for wait in drains:
            wait()

    def to_plane(k, src, dst, sent, rs=None):
        for j in range(1, NP):
            q = wrap(p + j, NP)
            rcopy(src(q), dst, k, zh * NP + q, s, rs).start()
        drains.append(lambda: bulk(sent, NP - 1, ssem.at[k]))

    def to_x(k, src, dst, many, rs=None):
        for j in range(1, NX):
            rcopy(src, dst, k, zh * NP + y * NX + wrap(x + j, NX), s, rs).start()
        drains.append(lambda: land(many, ssem.at[k]))

    def to_y(k, src, dst, many, rs=None):
        for j in range(1, NY):
            rcopy(src, dst, k, zh * NP + wrap(y + j, NY) * NX + x, s, rs).start()
        drains.append(lambda: land(many, ssem.at[k]))

    def to_tensor(k, src, dst, sent):
        for j in range(1, NT):
            q = wrap(s + j, NT)
            rcopy(src(q), dst, k, g, q).start()
        drains.append(lambda: bulk(sent, NT - 1, ssem.at[k]))

    barrier = pltpu.get_barrier_semaphore()

    def greet(dp, tensor):
        pl.semaphore_signal(
            barrier, inc=1, device_id={"dp": dp, "tensor": tensor}, device_id_type=MESH)
    for j in range(1, NT):
        greet(g, wrap(s + j, NT))
    for j in range(NT):
        greet((1 - zh) * NP + p, j)
    for j in range(1, NP):
        greet(zh * NP + wrap(p + j, NP), s)

    loads = []
    for z in range(NZ):
        for h in range(2):
            row = pl.multiple_of((2 * z + (c if h == 0 else 1 - c)) * CH, 16)
            loads.append(pltpu.make_async_copy(
                enc_hbm.at[pl.ds(row, CH)], E.at[h, pl.ds(z * CH, CH)], lsem.at[len(loads)]))
    n_enc = len(loads)
    for a, b in (
        (dec_hbm, DEC), (q_hbm, WQ.at[y, x]), (k_hbm, WK.at[y, x, :, 0:128]),
        (v_hbm, WK.at[y, x, :, 128:256]), (o_hbm, WB.at[y, x]),
    ):
        loads.append(pltpu.make_async_copy(a, b, lsem.at[len(loads)]))
    for cp in loads:
        cp.start()
    me_z = zh * NZ + zl
    COL[me_z] = resid[...]

    IDT[...] = jnp.concatenate([ids_ref[:, :R8], ids_ref[:, R8:]], axis=0)
    IDP[...] = IDT[...].T
    gi, gp = gain_in[...][None], gain_post[...][None]
    for j in range(NT):
        GIN[j:j + 1, :] = gi[:, j * CH:(j + 1) * CH]
        GPO[j:j + 1, :] = gp[:, j * CH:(j + 1) * CH]

    segc = jnp.broadcast_to(segs[...].astype(F32)[None], (128, T)).T
    SEGC[...] = jnp.concatenate(
        [segc[h * R8 + b * 8:h * R8 + b * 8 + 8] for b in range(NP) for h in range(2)], axis=0)
    mine = pl.ds(pl.multiple_of(p * 16, 16), 16)
    same = SEGC[mine, :][:, 0:1] == SEGC[...].T[0:1, :]
    row = lax.broadcasted_iota(jnp.int32, (16, 1), 0)
    col = lax.broadcasted_iota(jnp.int32, (1, T), 1)
    tr = (row >> 3) * R8 + p * 8 + (row & 7)
    tc = ((col >> 3) & 1) * R8 + (col >> 4) * 8 + (col & 7)
    allowed = same & (tc <= tr)
    pos = jnp.sum(jnp.where(same & (tc < tr), 1.0, 0.0), axis=1, keepdims=True)
    lane = lax.broadcasted_iota(jnp.int32, (1, 128), 1)
    inverse = jnp.exp((lane & 63).astype(F32) * (-2.0 * math.log(10000.0) / 128))
    ang = pos * inverse
    cosine = jnp.cos(ang)
    sine = jnp.where(lane < 64, -1.0, 1.0) * jnp.sin(ang)

    pl.semaphore_wait(barrier, 2 * NT - 1 + NP - 1)
    for j in range(1, 2 * NZ):
        z = wrap(me_z + j, 2 * NZ)
        far = jnp.where(z >= NZ, 1, 0)
        rcopy(resid, COL.at[me_z], 0, far * NP + p, (z - far * NZ) * 2 + c).start()
    drains.append(lambda: bulk(COL, 2 * NZ - 1, ssem.at[0]))

    @pl.loop(0, NP)
    def _(b):
        lo = (IDP[pl.ds(pl.multiple_of(b * 8, 8), 8), :] & 255).astype(F32).T
        cols = lax.broadcasted_iota(jnp.int32, (128, 256), 1).astype(F32)
        for i in range(8):
            B[b, pl.ds(i * 128, 128), :] = jnp.where(lo[:, i:i + 1] == cols, 1.0, 0.0).astype(BF16)

    bulk(COL, 2 * NZ - 1, rsem.at[0])
    halves = []
    for h in range(2):
        halves.append(jnp.concatenate(
            [COL[h * NZ + z].astype(F32) for z in range(NZ)], axis=1))
    X[0, y, x] = jnp.concatenate(halves, axis=0).astype(BF16)
    F2 = NZ * CH
    A, Bh = pl.ds(0, F2 // 2), pl.ds(F2 // 2, F2 // 2)

    def on(*where):
        rcopy(X.at[(0,) + where], X.at[(1,) + where], 2, g, sib, rsem.at[2]).start()
    own_a, own_b = X.at[0, y, x, :, A], X.at[0, y, x, :, Bh]
    row_a, col_b = X.at[0, y, :, :, A], X.at[0, :, x, :, Bh]
    own_as, own_bs = X.at[0, y, pl.ds(0, NX - 1), :, A], X.at[0, pl.ds(0, NY - 1), x, :, Bh]
    row_as, col_bs = X.at[0, pl.ds(0, NY - 1), :, :, A], X.at[0, :, pl.ds(0, NX - 1), :, Bh]
    to_x(1, own_a, own_a, own_as)
    to_y(17, own_b, own_b, own_bs)
    land(own_as, rsem.at[1])
    to_y(18, row_a, row_a, row_as, r2y.at[y])
    land(own_bs, rsem.at[17])
    to_x(19, col_b, col_b, col_bs, r2x.at[x])
    on(y, slice(None), slice(None), A)
    on(slice(None), x, slice(None), Bh)

    for cp in loads[n_enc + 1:]:
        cp.wait()
    lo, hi = pl.ds(0, 80), pl.ds(80, 64)
    nx, ny = pl.ds(0, NX - 1), pl.ds(0, NY - 1)
    own_q, own_k, own_ba, own_bb = WQ.at[y, x], WK.at[y, x], WB.at[y, x, lo], WB.at[y, x, hi]
    own_qs, own_ks, own_bas, own_bbs = WQ.at[y, nx], WK.at[ny, x], WB.at[y, nx, lo], WB.at[ny, x, hi]
    row_q, col_k, row_b, col_bb = WQ.at[y], WK.at[:, x], WB.at[y, :, lo], WB.at[:, x, hi]
    row_qs, col_ks, row_bs, col_bbs = WQ.at[ny], WK.at[:, nx], WB.at[ny, :, lo], WB.at[:, nx, hi]
    for j in range(1, max(NX, NY)):
        if j < NY:
            yy = wrap(y + NY - j, NY)
            land(row_a, r2y.at[yy])
            on(yy, slice(None), slice(None), A)
        if j < NX:
            xx = wrap(x + NX - j, NX)
            land(col_b, r2x.at[xx])
            on(slice(None), xx, slice(None), Bh)
    drains.append(lambda: land(X.at[0], ssem.at[2]))
    to_x(8, own_q, own_q, own_qs)
    to_y(9, own_k, own_k, own_ks)
    to_x(16, own_ba, own_ba, own_bas)
    to_y(20, own_bb, own_bb, own_bbs)

    for cp in loads[:n_enc]:
        cp.wait()
    pre = jnp.dot(X[0].reshape(T, F2), E[0], preferred_element_type=F32)
    land(X.at[1], rsem.at[2])
    pre = pre + jnp.dot(X[1].reshape(T, F2), E[1], preferred_element_type=F32)
    act = jnp.maximum(pre + enc_bias[...][None], 0.0).astype(BF16).astype(F32)

    act = act.reshape(NP, 2, 8, 256)
    a0 = act[:, 0].reshape(R8, 256)
    a1 = act[:, 1].reshape(R8, 256)
    rel = IDP[...] - (g * NT + s) * 256
    low = rel & 127
    left = lax.broadcasted_iota(jnp.int32, (R8, 128), 1) < 64

    def pick(h):
        return jnp.where(
            left,
            jnp.take_along_axis(a0[:, h * 128:(h + 1) * 128], low, axis=1),
            jnp.take_along_axis(a1[:, h * 128:(h + 1) * 128], low, axis=1))
    val = jnp.where(rel >= 128, pick(1), pick(0))
    val = jnp.where((rel >= 0) & (rel < 256), val, 0.0)
    VS[...] = val.reshape(NT, 8, 128).astype(BF16)
    first, NB = NT // 2 - 2, NT // 4
    middle = (s >= first) & (s < first + 4)
    part = pl.ds(jnp.where(middle, s - first, 0) * NB, NB)
    for k in range(4):
        @pl.when(s != first + k)
        def _():
            rcopy(VS.at[pl.ds(k * NB, NB)], VR.at[s], 3, g, first + k).start()
    land(own_qs, rsem.at[8])
    to_y(21, row_q, row_q, row_qs)
    land(own_ks, rsem.at[9])
    to_x(22, col_k, col_k, col_ks)

    @pl.when(middle)
    def _():
        VR[s] = VS[part]
        bulk(VR, NT - 1, rsem.at[3])
        VG[part] = jnp.sum(VR[...].astype(F32), axis=0).astype(BF16)
        for j in range(1, NT):
            rcopy(VG.at[part], VG.at[part], 4, g, wrap(s + j, NT)).start()

    def slots(sem, ref):
        @pl.when(middle)
        def _():
            bulk(ref, 3 * NB, sem)

        @pl.when(jnp.logical_not(middle))
        def _():
            bulk(ref, 4 * NB, sem)

    def spread():
        @pl.when(middle)
        def _():
            bulk(VR, NT - 1, ssem.at[4])
    drains.append(lambda: slots(ssem.at[3], VS))
    drains.append(spread)
    slots(rsem.at[4], VG)

    sub = lax.broadcasted_iota(jnp.int32, (8, 128), 0)
    lft = lax.broadcasted_iota(jnp.int32, (8, 128), 1) < 64
    @pl.loop(0, NP, unroll=4)
    def _(b):
        relb = IDP[pl.ds(pl.multiple_of(b * 8, 8), 8), :] - g * (NT * 256)
        vb = VG[b].astype(F32)
        hi = jnp.where(relb < 0, -1, relb >> 8)
        v0 = jnp.where(lft, vb, 0.0)
        v1 = vb - v0
        rows = []
        for h in range(NT):
            for vz in (v0, v1):
                d = jnp.where(hi == h, vz, 0.0)
                rows.append(jnp.concatenate([jnp.where(sub == i, d, 0.0) for i in range(8)], axis=1))
        lhs = jnp.concatenate(rows, axis=0).astype(BF16)
        sel = jnp.dot(lhs, B[b], preferred_element_type=F32).astype(BF16)
        S[:, pl.ds(pl.multiple_of(b * 16, 16), 16), :] = sel.reshape(NT, 16, 256)
    loads[n_enc].wait()
    rec = dot_nt(S[0], DEC[:, 0:256])
    for h in range(1, NT):
        rec = rec + dot_nt(S[h], DEC[:, h * 256:(h + 1) * 256])
    RS[...] = rec.reshape(NP, 16, CH)
    RR[p] = RS[p]
    to_plane(5, lambda q: RS.at[q], RR.at[p], RS)
    bulk(RR, NP - 1, rsem.at[5])
    land(own_bas, rsem.at[16])
    to_y(23, row_b, row_b, row_bs)
    land(own_bbs, rsem.at[20])
    to_x(24, col_bb, col_bb, col_bbs)
    ZS[...] = jnp.sum(RR[...], axis=0)
    zp = (1 - zh) * NP + p
    zc = rcopy(ZS, ZR, 6, zp, s)
    zc.start()
    drains.append(zc.wait_send)
    zc.wait_recv()
    spl = (ZS[...] + ZR[...] + dec_bias[...][None]).astype(BF16)
    SPF[...] = spl.astype(F32).reshape(2, 8, CH)
    SP[s] = spl

    rcopy(SP.at[s], SP.at[s], 10, g, sib, r7b.at[zl]).start()
    for j in range(1, NZ):
        rcopy(SP.at[s], SP.at[s], 7, g, 2 * wrap(zl + j, NZ) + c, r7.at[zl]).start()
    if NZ > 1:
        drains.append(lambda: bulk(SP, NZ - 1, ssem.at[7]))
    drains.append(lambda: bulk(SP, NZ, ssem.at[10]))
    for j in range(1, NZ):
        z = wrap(zl + NZ - j, NZ)
        there = SP.at[2 * z + c]
        pltpu.make_async_copy(there, there, r7.at[z]).wait()
        rcopy(there, there, 10, g, sib, r7b.at[z]).start()
    for z in range(NZ):
        pltpu.make_async_copy(SP.at[0], SP.at[0], r7b.at[z]).wait()

    ss = jnp.zeros((16, 1), F32)
    for j in range(NT):
        xj = SP[j].astype(F32)
        ss = ss + jnp.sum(xj * xj, axis=1, keepdims=True)
    rn = lax.rsqrt(ss / D + EPS)
    normed = []
    for j in range(NH):
        cj = zh * NH + j
        normed.append(SP[cj].astype(F32) * rn * GIN[pl.ds(cj, 1), :])
    normed = jnp.concatenate(normed, axis=1).astype(BF16)
    land(col_ks, rsem.at[22])
    YKS[...] = jnp.dot(normed, WK[...].reshape(NH * CH, 256), preferred_element_type=F32)
    kc = rcopy(YKS, YKR, 11, zp, s)
    kc.start()
    drains.append(kc.wait_send)
    land(row_qs, rsem.at[21])
    YQS[...] = jnp.dot(normed, WQ[...].reshape(NH * CH, 256), preferred_element_type=F32)
    qc = rcopy(YQS, YQR, 25, zp, s)
    qc.start()
    drains.append(qc.wait_send)

    def rot(v):
        return v * cosine + pltpu.roll(v, 64, 1) * sine
    kc.wait_recv()
    kv = YKS[...] + YKR[...]
    KV[p] = jnp.concatenate([rot(kv[:, 0:128]), kv[:, 128:256]], axis=1).astype(BF16)
    to_plane(12, lambda q: KV.at[p], KV.at[p], KV)
    qc.wait_recv()
    qs = YQS[...] + YQR[...]
    QB[...] = jnp.concatenate(
        [rot(qs[:, 0:128]) * QUERY_SCALE, rot(qs[:, 128:256]) * QUERY_SCALE], axis=1).astype(BF16)
    bulk(KV, NP - 1, rsem.at[12])

    kk = KV[:, :, 0:128].reshape(T, 128)
    vv = KV[:, :, 128:256].reshape(T, 128)
    for h in range(2):
        sc = dot_nt(QB[:, h * 128:(h + 1) * 128], kk)
        w = jnp.where(allowed, jnp.exp(SOFT_CAP * jnp.tanh(sc / SOFT_CAP)), 0.0)
        tot = jnp.sum(w, axis=1, keepdims=True)
        mixed = jnp.dot(w.astype(BF16), vv, preferred_element_type=F32)
        HO[:, h * 128:(h + 1) * 128] = (mixed / tot).astype(BF16)
    land(row_bs, rsem.at[23])
    land(col_bbs, rsem.at[24])
    wb = WB[...].reshape(NH * CH, 256)
    for j in range(NH):
        o = dot_nt(HO[...], wb[j * CH:(j + 1) * CH])
        OSD[0, j] = o[:8]
        OSD[1, j] = o[8:]

    oc = rcopy(OSD.at[1 - c], OSR, 13, g, sib)
    oc.start()
    drains.append(oc.wait_send)
    oc.wait_recv()
    OSS[...] = OSD[c] + OSR[...]
    own = (c == zh) & (s // NH == zh)
    for j in range(NH):
        here = (c == zh) & (zh * NH + j == s)

        @pl.when(here)
        def _():
            OR[zl] = OSS[j]

        @pl.when(jnp.logical_not(here))
        def _():
            rcopy(OSS.at[j], OR.at[zl], 14, c * NP + p, zh * NH + j).start()

    def bulk_own(ref, sem):
        @pl.when(own)
        def _():
            if NZ > 1:
                bulk(ref, NZ - 1, sem)

        @pl.when(jnp.logical_not(own))
        def _():
            bulk(ref, NZ, sem)
    drains.append(lambda: bulk_own(OSS, ssem.at[14]))
    bulk_own(OR, rsem.at[14])
    att = jnp.sum(OR[...], axis=0)
    diag = lax.broadcasted_iota(jnp.int32, (8, 128), 0) == lax.broadcasted_iota(jnp.int32, (8, 128), 1)
    NR[s] = jnp.sum(jnp.where(diag, jnp.sum(att * att, axis=1, keepdims=True), 0.0), axis=0, keepdims=True)
    to_tensor(15, lambda q: NR.at[s], NR.at[s], NR)
    bulk(NR, NT - 1, rsem.at[15])
    tot = jnp.sum(jnp.where(diag, jnp.sum(NR[...], axis=0), 0.0), axis=1, keepdims=True)
    post = att * lax.rsqrt(tot / D + EPS) * GPO[pl.ds(s, 1), :]
    out_ref[...] = (SPF[zh] + post).astype(BF16)
    drain()


def local(mesh, resid, enc, enc_bias, ids, dec, dec_bias, segs, gin, gpo, qw, kw, vw, ow):
    NT = mesh.shape["tensor"]
    NP = mesh.shape["dp"] // 2
    assert NT == NP
    T, CH, NZ = 16 * NP, resid.shape[1], NT // 2
    HC = CH // 2
    NX = 1 << (NP.bit_length() // 2)
    NY = NP // NX
    V = pltpu.VMEM
    scratch = [
        V((2, NZ * CH, 256), BF16), V(dec.shape[::-1], BF16), V((NY, NX, HC, 256), BF16),
        V((NY, NX, HC, 256), BF16), V((NY, NX, HC, 256), BF16),
        V((2 * NZ, 8, CH), BF16), V((2, NY, NX, 16, NZ * CH), BF16), V((128, 8 * NP), jnp.int32),
        V((8 * NP, 128), jnp.int32), V((NP, 1024, 256), BF16),
        V((NT, 8, 128), BF16), V((NT, NT // 4, 8, 128), BF16), V((NT, 8, 128), BF16), V((NT, T, 256), BF16),
        V((NP, 16, CH), F32), V((NP, 16, CH), F32), V((16, CH), F32), V((16, CH), F32),
        V((2, 8, CH), F32), V((NT, 16, CH), BF16), V((NT, CH), F32), V((NT, CH), F32),
        V((16, 256), F32), V((16, 256), F32), V((16, 256), F32), V((16, 256), F32), V((16, 256), BF16), V((NP, 16, 256), BF16),
        V((T, 128), F32), V((16, 256), BF16),
        V((2, NZ, 8, CH), F32), V((NZ, 8, CH), F32), V((NZ, 8, CH), F32), V((NZ, 8, CH), F32),
        V((NT, 1, 128), F32),
        pltpu.SemaphoreType.DMA((2 * NZ + 5,)), pltpu.SemaphoreType.DMA((26,)),
        pltpu.SemaphoreType.DMA((26,)), pltpu.SemaphoreType.DMA((NX,)), pltpu.SemaphoreType.DMA((NY,)),
        pltpu.SemaphoreType.DMA((NZ,)), pltpu.SemaphoreType.DMA((NZ,)),
    ]
    vm = pl.BlockSpec(memory_space=V)
    hbm = pl.BlockSpec(memory_space=pl.ANY)
    return pl.pallas_call(
        lambda *refs: kernel(NP, NT, NX, NY, *refs),
        out_shape=jax.ShapeDtypeStruct((8, CH), BF16),
        in_specs=[vm, hbm, vm, vm, hbm, vm, vm, vm, vm, hbm, hbm, hbm, hbm],
        out_specs=vm,
        scratch_shapes=scratch,
        compiler_params=pltpu.CompilerParams(
            collective_id=0, has_side_effects=True, vmem_limit_bytes=56 * 1024 * 1024),
    )(resid, enc, enc_bias, ids.T, dec.T, dec_bias, segs, gin, gpo, qw, kw, vw, ow.T)


def solution(mesh):
    return jax.shard_map(
        lambda *args: local(mesh, *args),
        mesh=mesh,
        in_specs=(
            P("dp", "tensor"),
            P(None, ("dp", "tensor")),
            P(("dp", "tensor")),
            P(),
            P("dp", "tensor"),
            P("tensor"),
            P(),
            P(),
            P(),
            P("dp", "tensor"),
            P("dp", "tensor"),
            P("dp", "tensor"),
            P("tensor", "dp"),
        ),
        out_specs=P("dp", "tensor"),
        check_vma=False,
    )
```

```python
import math

import jax
import jax.numpy as jnp
from jax import lax
from jax.experimental import pallas as pl
from jax.experimental.pallas import tpu as pltpu
from jax.sharding import PartitionSpec as P

QUERY_SCALE = 144.0 ** (-0.5)
SOFT_CAP = 50.0
EPS = 1e-06
MESH = pl.DeviceIdType.MESH
F32 = jnp.float32
BF16 = jnp.bfloat16


def dot_nt(a, b):
    return lax.dot_general(a, b, (((1,), (1,)), ((), ())), preferred_element_type=F32)


def kernel(
    NP, NT, NX, NY,
    resid, enc_hbm, enc_bias, ids_ref, dec_hbm, dec_bias, segs, gain_in, gain_post,
    q_hbm, k_hbm, v_hbm, o_hbm,
    out_ref,
    E, DEC, WQ, WK, WB,
    COL, X, IDT, IDP, B, VS, VR, VG, S,
    RS, RR, ZS, ZR, SPF, SP, GIN, GPO, YKS, YKR, YQS, YQR, QB, KV,
    SEGC, HO, OSD, OSR, OSS, OR, NR,
    lsem, ssem, rsem, r2x, r2y, r7, r7b,
):
    T = 16 * NP
    R8 = 8 * NP
    NZ = NT // 2
    NH = NT // 2
    CH = resid.shape[1]
    D = NT * CH
    g = lax.axis_index("dp")
    s = lax.axis_index("tensor")
    zh = g // NP
    p = g % NP
    zl = s // 2
    c = s % 2
    x = p % NX
    y = p // NX
    sib = s + 1 - 2 * c

    def wrap(i, n):
        return jnp.where(i >= n, i - n, i)

    def rcopy(src, dst, k, dp, tensor, rs=None):
        return pltpu.make_async_remote_copy(
            src_ref=src, dst_ref=dst, send_sem=ssem.at[k],
            recv_sem=rsem.at[k] if rs is None else rs,
            device_id={"dp": dp, "tensor": tensor}, device_id_type=MESH)

    drains = []

    def bulk(ref, n, sem):
        d = ref.at[pl.ds(0, n)]
        pltpu.make_async_copy(d, d, sem).wait()

    def land(ref, sem):
        pltpu.make_async_copy(ref, ref, sem).wait()

    def drain():
        for wait in drains:
            wait()

    def to_plane(k, src, dst, sent, rs=None):
        for j in range(1, NP):
            q = wrap(p + j, NP)
            rcopy(src(q), dst, k, zh * NP + q, s, rs).start()
        drains.append(lambda: bulk(sent, NP - 1, ssem.at[k]))

    def to_x(k, src, dst, many, rs=None):
        for j in range(1, NX):
            rcopy(src, dst, k, zh * NP + y * NX + wrap(x + j, NX), s, rs).start()
        drains.append(lambda: land(many, ssem.at[k]))

    def to_y(k, src, dst, many, rs=None):
        for j in range(1, NY):
            rcopy(src, dst, k, zh * NP + wrap(y + j, NY) * NX + x, s, rs).start()
        drains.append(lambda: land(many, ssem.at[k]))

    def to_tensor(k, src, dst, sent):
        for j in range(1, NT):
            q = wrap(s + j, NT)
            rcopy(src(q), dst, k, g, q).start()
        drains.append(lambda: bulk(sent, NT - 1, ssem.at[k]))

    barrier = pltpu.get_barrier_semaphore()

    def greet(dp, tensor):
        pl.semaphore_signal(
            barrier, inc=1, device_id={"dp": dp, "tensor": tensor}, device_id_type=MESH)
    for j in range(1, NT):
        greet(g, wrap(s + j, NT))
    for j in range(NT):
        greet((1 - zh) * NP + p, j)
    for j in range(1, NP):
        greet(zh * NP + wrap(p + j, NP), s)

    loads = []
    for z in range(NZ):
        for h in range(2):
            row = pl.multiple_of((2 * z + (c if h == 0 else 1 - c)) * CH, 16)
            loads.append(pltpu.make_async_copy(
                enc_hbm.at[pl.ds(row, CH)], E.at[h, pl.ds(z * CH, CH)], lsem.at[len(loads)]))
    n_enc = len(loads)
    for a, b in (
        (dec_hbm, DEC), (q_hbm, WQ.at[y, x]), (k_hbm, WK.at[y, x, :, 0:128]),
        (v_hbm, WK.at[y, x, :, 128:256]), (o_hbm, WB.at[y, x]),
    ):
        loads.append(pltpu.make_async_copy(a, b, lsem.at[len(loads)]))
    for cp in loads:
        cp.start()
    me_z = zh * NZ + zl
    COL[me_z] = resid[...]

    IDT[...] = jnp.concatenate([ids_ref[:, :R8], ids_ref[:, R8:]], axis=0)
    IDP[...] = IDT[...].T
    gi, gp = gain_in[...][None], gain_post[...][None]
    for j in range(NT):
        GIN[j:j + 1, :] = gi[:, j * CH:(j + 1) * CH]
        GPO[j:j + 1, :] = gp[:, j * CH:(j + 1) * CH]

    segc = jnp.broadcast_to(segs[...].astype(F32)[None], (128, T)).T
    SEGC[...] = jnp.concatenate(
        [segc[h * R8 + b * 8:h * R8 + b * 8 + 8] for b in range(NP) for h in range(2)], axis=0)
    mine = pl.ds(pl.multiple_of(p * 16, 16), 16)
    same = SEGC[mine, :][:, 0:1] == SEGC[...].T[0:1, :]
    row = lax.broadcasted_iota(jnp.int32, (16, 1), 0)
    col = lax.broadcasted_iota(jnp.int32, (1, T), 1)
    tr = (row >> 3) * R8 + p * 8 + (row & 7)
    tc = ((col >> 3) & 1) * R8 + (col >> 4) * 8 + (col & 7)
    allowed = same & (tc <= tr)
    pos = jnp.sum(jnp.where(same & (tc < tr), 1.0, 0.0), axis=1, keepdims=True)
    lane = lax.broadcasted_iota(jnp.int32, (1, 128), 1)
    inverse = jnp.exp((lane & 63).astype(F32) * (-2.0 * math.log(10000.0) / 128))
    ang = pos * inverse
    cosine = jnp.cos(ang)
    sine = jnp.where(lane < 64, -1.0, 1.0) * jnp.sin(ang)

    pl.semaphore_wait(barrier, 2 * NT - 1 + NP - 1)
    for j in range(1, 2 * NZ):
        z = wrap(me_z + j, 2 * NZ)
        far = jnp.where(z >= NZ, 1, 0)
        rcopy(resid, COL.at[me_z], 0, far * NP + p, (z - far * NZ) * 2 + c).start()
    drains.append(lambda: bulk(COL, 2 * NZ - 1, ssem.at[0]))

    @pl.loop(0, NP)
    def _(b):
        lo = (IDP[pl.ds(pl.multiple_of(b * 8, 8), 8), :] & 255).astype(F32).T
        cols = lax.broadcasted_iota(jnp.int32, (128, 256), 1).astype(F32)
        for i in range(8):
            B[b, pl.ds(i * 128, 128), :] = jnp.where(lo[:, i:i + 1] == cols, 1.0, 0.0).astype(BF16)

    bulk(COL, 2 * NZ - 1, rsem.at[0])
    halves = []
    for h in range(2):
        halves.append(jnp.concatenate(
            [COL[h * NZ + z].astype(F32) for z in range(NZ)], axis=1))
    X[0, y, x] = jnp.concatenate(halves, axis=0).astype(BF16)
    F2 = NZ * CH
    A, Bh = pl.ds(0, F2 // 2), pl.ds(F2 // 2, F2 // 2)

    def on(*where):
        rcopy(X.at[(0,) + where], X.at[(1,) + where], 2, g, sib, rsem.at[2]).start()
    own_a, own_b = X.at[0, y, x, :, A], X.at[0, y, x, :, Bh]
    row_a, col_b = X.at[0, y, :, :, A], X.at[0, :, x, :, Bh]
    own_as, own_bs = X.at[0, y, pl.ds(0, NX - 1), :, A], X.at[0, pl.ds(0, NY - 1), x, :, Bh]
    row_as, col_bs = X.at[0, pl.ds(0, NY - 1), :, :, A], X.at[0, :, pl.ds(0, NX - 1), :, Bh]
    to_x(1, own_a, own_a, own_as)
    to_y(17, own_b, own_b, own_bs)
    land(own_as, rsem.at[1])
    to_y(18, row_a, row_a, row_as, r2y.at[y])
    land(own_bs, rsem.at[17])
    to_x(19, col_b, col_b, col_bs, r2x.at[x])
    on(y, slice(None), slice(None), A)
    on(slice(None), x, slice(None), Bh)

    for cp in loads[n_enc + 1:]:
        cp.wait()
    lo, hi = pl.ds(0, 80), pl.ds(80, 64)
    nx, ny = pl.ds(0, NX - 1), pl.ds(0, NY - 1)
    own_q, own_k, own_ba, own_bb = WQ.at[y, x], WK.at[y, x], WB.at[y, x, lo], WB.at[y, x, hi]
    own_qs, own_ks, own_bas, own_bbs = WQ.at[y, nx], WK.at[ny, x], WB.at[y, nx, lo], WB.at[ny, x, hi]
    row_q, col_k, row_b, col_bb = WQ.at[y], WK.at[:, x], WB.at[y, :, lo], WB.at[:, x, hi]
    row_qs, col_ks, row_bs, col_bbs = WQ.at[ny], WK.at[:, nx], WB.at[ny, :, lo], WB.at[:, nx, hi]
    for j in range(1, max(NX, NY)):
        if j < NY:
            yy = wrap(y + NY - j, NY)
            land(row_a, r2y.at[yy])
            on(yy, slice(None), slice(None), A)
        if j < NX:
            xx = wrap(x + NX - j, NX)
            land(col_b, r2x.at[xx])
            on(slice(None), xx, slice(None), Bh)
    drains.append(lambda: land(X.at[0], ssem.at[2]))
    to_x(8, own_q, own_q, own_qs)
    to_y(9, own_k, own_k, own_ks)
    to_x(16, own_ba, own_ba, own_bas)
    to_y(20, own_bb, own_bb, own_bbs)

    for cp in loads[:n_enc]:
        cp.wait()
    pre = jnp.dot(X[0].reshape(T, F2), E[0], preferred_element_type=F32)
    land(X.at[1], rsem.at[2])
    pre = pre + jnp.dot(X[1].reshape(T, F2), E[1], preferred_element_type=F32)
    act = jnp.maximum(pre + enc_bias[...][None], 0.0).astype(BF16).astype(F32)

    act = act.reshape(NP, 2, 8, 256)
    a0 = act[:, 0].reshape(R8, 256)
    a1 = act[:, 1].reshape(R8, 256)
    rel = IDP[...] - (g * NT + s) * 256
    low = rel & 127
    left = lax.broadcasted_iota(jnp.int32, (R8, 128), 1) < 64

    def pick(h):
        return jnp.where(
            left,
            jnp.take_along_axis(a0[:, h * 128:(h + 1) * 128], low, axis=1),
            jnp.take_along_axis(a1[:, h * 128:(h + 1) * 128], low, axis=1))
    val = jnp.where(rel >= 128, pick(1), pick(0))
    val = jnp.where((rel >= 0) & (rel < 256), val, 0.0)
    VS[...] = val.reshape(NT, 8, 128).astype(BF16)
    first, NB = NT // 2 - 2, NT // 4
    middle = (s >= first) & (s < first + 4)
    part = pl.ds(jnp.where(middle, s - first, 0) * NB, NB)
    for k in range(4):
        @pl.when(s != first + k)
        def _():
            rcopy(VS.at[pl.ds(k * NB, NB)], VR.at[s], 3, g, first + k).start()
    land(own_qs, rsem.at[8])
    to_y(21, row_q, row_q, row_qs)
    land(own_ks, rsem.at[9])
    to_x(22, col_k, col_k, col_ks)

    @pl.when(middle)
    def _():
        VR[s] = VS[part]
        bulk(VR, NT - 1, rsem.at[3])
        VG[part] = jnp.sum(VR[...].astype(F32), axis=0).astype(BF16)
        for j in range(1, NT):
            rcopy(VG.at[part], VG.at[part], 4, g, wrap(s + j, NT)).start()

    def slots(sem, ref):
        @pl.when(middle)
        def _():
            bulk(ref, 3 * NB, sem)

        @pl.when(jnp.logical_not(middle))
        def _():
            bulk(ref, 4 * NB, sem)

    def spread():
        @pl.when(middle)
        def _():
            bulk(VR, NT - 1, ssem.at[4])
    drains.append(lambda: slots(ssem.at[3], VS))
    drains.append(spread)
    slots(rsem.at[4], VG)

    sub = lax.broadcasted_iota(jnp.int32, (8, 128), 0)
    lft = lax.broadcasted_iota(jnp.int32, (8, 128), 1) < 64
    @pl.loop(0, NP, unroll=8 if NP % 8 == 0 else 1)
    def _(b):
        relb = IDP[pl.ds(pl.multiple_of(b * 8, 8), 8), :] - g * (NT * 256)
        vb = VG[b].astype(F32)
        hi = jnp.where(relb < 0, -1, relb >> 8)
        v0 = jnp.where(lft, vb, 0.0)
        v1 = vb - v0
        rows = []
        for h in range(NT):
            for vz in (v0, v1):
                d = jnp.where(hi == h, vz, 0.0)
                rows.append(jnp.concatenate([jnp.where(sub == i, d, 0.0) for i in range(8)], axis=1))
        lhs = jnp.concatenate(rows, axis=0).astype(BF16)
        sel = jnp.dot(lhs, B[b], preferred_element_type=F32).astype(BF16)
        S[:, pl.ds(pl.multiple_of(b * 16, 16), 16), :] = sel.reshape(NT, 16, 256)
    loads[n_enc].wait()
    rec = dot_nt(S[0], DEC[:, 0:256])
    for h in range(1, NT):
        rec = rec + dot_nt(S[h], DEC[:, h * 256:(h + 1) * 256])
    RS[...] = rec.reshape(NP, 16, CH)
    RR[p] = RS[p]
    to_plane(5, lambda q: RS.at[q], RR.at[p], RS)
    bulk(RR, NP - 1, rsem.at[5])
    land(own_bas, rsem.at[16])
    to_y(23, row_b, row_b, row_bs)
    land(own_bbs, rsem.at[20])
    to_x(24, col_bb, col_bb, col_bbs)
    ZS[...] = jnp.sum(RR[...], axis=0)
    zp = (1 - zh) * NP + p
    zc = rcopy(ZS, ZR, 6, zp, s)
    zc.start()
    drains.append(zc.wait_send)
    zc.wait_recv()
    spl = (ZS[...] + ZR[...] + dec_bias[...][None]).astype(BF16)
    SPF[...] = spl.astype(F32).reshape(2, 8, CH)
    SP[s] = spl

    rcopy(SP.at[s], SP.at[s], 10, g, sib, r7b.at[zl]).start()
    for j in range(1, NZ):
        rcopy(SP.at[s], SP.at[s], 7, g, 2 * wrap(zl + j, NZ) + c, r7.at[zl]).start()
    if NZ > 1:
        drains.append(lambda: bulk(SP, NZ - 1, ssem.at[7]))
    drains.append(lambda: bulk(SP, NZ, ssem.at[10]))
    for j in range(1, NZ):
        z = wrap(zl + NZ - j, NZ)
        there = SP.at[2 * z + c]
        pltpu.make_async_copy(there, there, r7.at[z]).wait()
        rcopy(there, there, 10, g, sib, r7b.at[z]).start()
    for z in range(NZ):
        pltpu.make_async_copy(SP.at[0], SP.at[0], r7b.at[z]).wait()

    ss = jnp.zeros((16, 1), F32)
    for j in range(NT):
        xj = SP[j].astype(F32)
        ss = ss + jnp.sum(xj * xj, axis=1, keepdims=True)
    rn = lax.rsqrt(ss / D + EPS)
    normed = []
    for j in range(NH):
        cj = zh * NH + j
        normed.append(SP[cj].astype(F32) * rn * GIN[pl.ds(cj, 1), :])
    normed = jnp.concatenate(normed, axis=1).astype(BF16)
    land(col_ks, rsem.at[22])
    YKS[...] = jnp.dot(normed, WK[...].reshape(NH * CH, 256), preferred_element_type=F32)
    kc = rcopy(YKS, YKR, 11, zp, s)
    kc.start()
    drains.append(kc.wait_send)
    land(row_qs, rsem.at[21])
    YQS[...] = jnp.dot(normed, WQ[...].reshape(NH * CH, 256), preferred_element_type=F32)
    qc = rcopy(YQS, YQR, 25, zp, s)
    qc.start()
    drains.append(qc.wait_send)

    def rot(v):
        return v * cosine + pltpu.roll(v, 64, 1) * sine
    kc.wait_recv()
    kv = YKS[...] + YKR[...]
    KV[p] = jnp.concatenate([rot(kv[:, 0:128]), kv[:, 128:256]], axis=1).astype(BF16)
    to_plane(12, lambda q: KV.at[p], KV.at[p], KV)
    qc.wait_recv()
    qs = YQS[...] + YQR[...]
    QB[...] = jnp.concatenate(
        [rot(qs[:, 0:128]) * QUERY_SCALE, rot(qs[:, 128:256]) * QUERY_SCALE], axis=1).astype(BF16)
    bulk(KV, NP - 1, rsem.at[12])

    kk = KV[:, :, 0:128].reshape(T, 128)
    vv = KV[:, :, 128:256].reshape(T, 128)
    for h in range(2):
        sc = dot_nt(QB[:, h * 128:(h + 1) * 128], kk)
        w = jnp.where(allowed, jnp.exp(SOFT_CAP * jnp.tanh(sc / SOFT_CAP)), 0.0)
        tot = jnp.sum(w, axis=1, keepdims=True)
        mixed = jnp.dot(w.astype(BF16), vv, preferred_element_type=F32)
        HO[:, h * 128:(h + 1) * 128] = (mixed / tot).astype(BF16)
    land(row_bs, rsem.at[23])
    land(col_bbs, rsem.at[24])
    wb = WB[...].reshape(NH * CH, 256)
    for j in range(NH):
        o = dot_nt(HO[...], wb[j * CH:(j + 1) * CH])
        OSD[0, j] = o[:8]
        OSD[1, j] = o[8:]

    oc = rcopy(OSD.at[1 - c], OSR, 13, g, sib)
    oc.start()
    drains.append(oc.wait_send)
    oc.wait_recv()
    OSS[...] = (OSD[c] + OSR[...]).astype(BF16)
    own = (c == zh) & (s // NH == zh)
    for j in range(NH):
        here = (c == zh) & (zh * NH + j == s)

        @pl.when(here)
        def _():
            OR[zl] = OSS[j]

        @pl.when(jnp.logical_not(here))
        def _():
            rcopy(OSS.at[j], OR.at[zl], 14, c * NP + p, zh * NH + j).start()

    def bulk_own(ref, sem):
        @pl.when(own)
        def _():
            if NZ > 1:
                bulk(ref, NZ - 1, sem)

        @pl.when(jnp.logical_not(own))
        def _():
            bulk(ref, NZ, sem)
    drains.append(lambda: bulk_own(OSS, ssem.at[14]))
    bulk_own(OR, rsem.at[14])
    att = jnp.sum(OR[...].astype(F32), axis=0)
    diag = lax.broadcasted_iota(jnp.int32, (8, 128), 0) == lax.broadcasted_iota(jnp.int32, (8, 128), 1)
    NR[s] = jnp.sum(jnp.where(diag, jnp.sum(att * att, axis=1, keepdims=True), 0.0), axis=0, keepdims=True)
    to_tensor(15, lambda q: NR.at[s], NR.at[s], NR)
    bulk(NR, NT - 1, rsem.at[15])
    tot = jnp.sum(jnp.where(diag, jnp.sum(NR[...], axis=0), 0.0), axis=1, keepdims=True)
    post = att * lax.rsqrt(tot / D + EPS) * GPO[pl.ds(s, 1), :]
    out_ref[...] = (SPF[zh] + post).astype(BF16)
    drain()


def local(mesh, resid, enc, enc_bias, ids, dec, dec_bias, segs, gin, gpo, qw, kw, vw, ow):
    NT = mesh.shape["tensor"]
    NP = mesh.shape["dp"] // 2
    assert NT == NP
    T, CH, NZ = 16 * NP, resid.shape[1], NT // 2
    HC = CH // 2
    NX = 1 << (NP.bit_length() // 2)
    NY = NP // NX
    V = pltpu.VMEM
    scratch = [
        V((2, NZ * CH, 256), BF16), V(dec.shape[::-1], BF16), V((NY, NX, HC, 256), BF16),
        V((NY, NX, HC, 256), BF16), V((NY, NX, HC, 256), BF16),
        V((2 * NZ, 8, CH), BF16), V((2, NY, NX, 16, NZ * CH), BF16), V((128, 8 * NP), jnp.int32),
        V((8 * NP, 128), jnp.int32), V((NP, 1024, 256), BF16),
        V((NT, 8, 128), BF16), V((NT, NT // 4, 8, 128), BF16), V((NT, 8, 128), BF16), V((NT, T, 256), BF16),
        V((NP, 16, CH), F32), V((NP, 16, CH), F32), V((16, CH), F32), V((16, CH), F32),
        V((2, 8, CH), F32), V((NT, 16, CH), BF16), V((NT, CH), F32), V((NT, CH), F32),
        V((16, 256), F32), V((16, 256), F32), V((16, 256), F32), V((16, 256), F32), V((16, 256), BF16), V((NP, 16, 256), BF16),
        V((T, 128), F32), V((16, 256), BF16),
        V((2, NZ, 8, CH), F32), V((NZ, 8, CH), F32), V((NZ, 8, CH), BF16), V((NZ, 8, CH), BF16),
        V((NT, 1, 128), F32),
        pltpu.SemaphoreType.DMA((2 * NZ + 5,)), pltpu.SemaphoreType.DMA((26,)),
        pltpu.SemaphoreType.DMA((26,)), pltpu.SemaphoreType.DMA((NX,)), pltpu.SemaphoreType.DMA((NY,)),
        pltpu.SemaphoreType.DMA((NZ,)), pltpu.SemaphoreType.DMA((NZ,)),
    ]
    vm = pl.BlockSpec(memory_space=V)
    hbm = pl.BlockSpec(memory_space=pl.ANY)
    return pl.pallas_call(
        lambda *refs: kernel(NP, NT, NX, NY, *refs),
        out_shape=jax.ShapeDtypeStruct((8, CH), BF16),
        in_specs=[vm, hbm, vm, vm, hbm, vm, vm, vm, vm, hbm, hbm, hbm, hbm],
        out_specs=vm,
        scratch_shapes=scratch,
        compiler_params=pltpu.CompilerParams(
            collective_id=0, has_side_effects=True, vmem_limit_bytes=56 * 1024 * 1024),
    )(resid, enc, enc_bias, ids.T, dec.T, dec_bias, segs, gin, gpo, qw, kw, vw, ow.T)


def solution(mesh):
    return jax.shard_map(
        lambda *args: local(mesh, *args),
        mesh=mesh,
        in_specs=(
            P("dp", "tensor"),
            P(None, ("dp", "tensor")),
            P(("dp", "tensor")),
            P(),
            P("dp", "tensor"),
            P("tensor"),
            P(),
            P(),
            P(),
            P("dp", "tensor"),
            P("dp", "tensor"),
            P("dp", "tensor"),
            P("tensor", "dp"),
        ),
        out_specs=P("dp", "tensor"),
        check_vma=False,
    )
```

```python
import math

import jax
import jax.numpy as jnp
from jax import lax
from jax.experimental import pallas as pl
from jax.experimental.pallas import tpu as pltpu
from jax.sharding import PartitionSpec as P

QUERY_SCALE = 144.0 ** (-0.5)
SOFT_CAP = 50.0
EPS = 1e-06
MESH = pl.DeviceIdType.MESH
F32 = jnp.float32
BF16 = jnp.bfloat16


def dot_nt(a, b):
    return lax.dot_general(a, b, (((1,), (1,)), ((), ())), preferred_element_type=F32)


def kernel(
    NP, NT, NX, NY,
    resid, enc_hbm, enc_bias, ids_ref, dec_hbm, dec_bias, segs, gain_in, gain_post,
    q_hbm, k_hbm, v_hbm, o_hbm,
    out_ref,
    E, DEC, WQ, WK, WB,
    COL, X, IDT, IDP, B, VS, VR, VG, S,
    RS, RR, ZS, ZR, SPF, SP, GIN, GPO, YKS, YKR, YQS, YQR, QB, KV,
    SEGC, HO, OSD, OSR, OSS, OR, NR,
    lsem, ssem, rsem, r2x, r2y, r7, r7b,
):
    T = 16 * NP
    R8 = 8 * NP
    NZ = NT // 2
    NH = NT // 2
    CH = resid.shape[1]
    D = NT * CH
    g = lax.axis_index("dp")
    s = lax.axis_index("tensor")
    zh = g // NP
    p = g % NP
    zl = s // 2
    c = s % 2
    x = p % NX
    y = p // NX
    sib = s + 1 - 2 * c

    def wrap(i, n):
        return jnp.where(i >= n, i - n, i)

    def rcopy(src, dst, k, dp, tensor, rs=None):
        return pltpu.make_async_remote_copy(
            src_ref=src, dst_ref=dst, send_sem=ssem.at[k],
            recv_sem=rsem.at[k] if rs is None else rs,
            device_id={"dp": dp, "tensor": tensor}, device_id_type=MESH)

    drains = []

    def bulk(ref, n, sem):
        d = ref.at[pl.ds(0, n)]
        pltpu.make_async_copy(d, d, sem).wait()

    def land(ref, sem):
        pltpu.make_async_copy(ref, ref, sem).wait()

    def drain():
        for wait in drains:
            wait()

    def to_plane(k, src, dst, sent, rs=None):
        for j in range(1, NP):
            q = wrap(p + j, NP)
            rcopy(src(q), dst, k, zh * NP + q, s, rs).start()
        drains.append(lambda: bulk(sent, NP - 1, ssem.at[k]))

    def to_x(k, src, dst, many, rs=None):
        for j in range(1, NX):
            rcopy(src, dst, k, zh * NP + y * NX + wrap(x + j, NX), s, rs).start()
        drains.append(lambda: land(many, ssem.at[k]))

    def to_y(k, src, dst, many, rs=None):
        for j in range(1, NY):
            rcopy(src, dst, k, zh * NP + wrap(y + j, NY) * NX + x, s, rs).start()
        drains.append(lambda: land(many, ssem.at[k]))

    def to_tensor(k, src, dst, sent):
        for j in range(1, NT):
            q = wrap(s + j, NT)
            rcopy(src(q), dst, k, g, q).start()
        drains.append(lambda: bulk(sent, NT - 1, ssem.at[k]))

    barrier = pltpu.get_barrier_semaphore()

    def greet(dp, tensor):
        pl.semaphore_signal(
            barrier, inc=1, device_id={"dp": dp, "tensor": tensor}, device_id_type=MESH)
    for j in range(1, NT):
        greet(g, wrap(s + j, NT))
    for j in range(NT):
        greet((1 - zh) * NP + p, j)
    for j in range(1, NP):
        greet(zh * NP + wrap(p + j, NP), s)

    loads = []
    for z in range(NZ):
        for h in range(2):
            row = pl.multiple_of((2 * z + (c if h == 0 else 1 - c)) * CH, 16)
            loads.append(pltpu.make_async_copy(
                enc_hbm.at[pl.ds(row, CH)], E.at[h, pl.ds(z * CH, CH)], lsem.at[len(loads)]))
    n_enc = len(loads)
    for a, b in (
        (dec_hbm, DEC), (q_hbm, WQ.at[y, x]), (k_hbm, WK.at[y, x, :, 0:128]),
        (v_hbm, WK.at[y, x, :, 128:256]), (o_hbm, WB.at[y, x]),
    ):
        loads.append(pltpu.make_async_copy(a, b, lsem.at[len(loads)]))
    for cp in loads:
        cp.start()
    me_z = zh * NZ + zl
    COL[me_z] = resid[...]

    IDT[...] = jnp.concatenate([ids_ref[:, :R8], ids_ref[:, R8:]], axis=0)
    IDP[...] = IDT[...].T
    gi, gp = gain_in[...][None], gain_post[...][None]
    for j in range(NT):
        GIN[j:j + 1, :] = gi[:, j * CH:(j + 1) * CH]
        GPO[j:j + 1, :] = gp[:, j * CH:(j + 1) * CH]

    segc = jnp.broadcast_to(segs[...].astype(F32)[None], (128, T)).T
    SEGC[...] = jnp.concatenate(
        [segc[h * R8 + b * 8:h * R8 + b * 8 + 8] for b in range(NP) for h in range(2)], axis=0)
    mine = pl.ds(pl.multiple_of(p * 16, 16), 16)
    same = SEGC[mine, :][:, 0:1] == SEGC[...].T[0:1, :]
    row = lax.broadcasted_iota(jnp.int32, (16, 1), 0)
    col = lax.broadcasted_iota(jnp.int32, (1, T), 1)
    tr = (row >> 3) * R8 + p * 8 + (row & 7)
    tc = ((col >> 3) & 1) * R8 + (col >> 4) * 8 + (col & 7)
    allowed = same & (tc <= tr)
    pos = jnp.sum(jnp.where(same & (tc < tr), 1.0, 0.0), axis=1, keepdims=True)
    lane = lax.broadcasted_iota(jnp.int32, (1, 128), 1)
    inverse = jnp.exp((lane & 63).astype(F32) * (-2.0 * math.log(10000.0) / 128))
    ang = pos * inverse
    cosine = jnp.cos(ang)
    sine = jnp.where(lane < 64, -1.0, 1.0) * jnp.sin(ang)

    pl.semaphore_wait(barrier, 2 * NT - 1 + NP - 1)
    for j in range(1, 2 * NZ):
        z = wrap(me_z + j, 2 * NZ)
        far = jnp.where(z >= NZ, 1, 0)
        rcopy(resid, COL.at[me_z], 0, far * NP + p, (z - far * NZ) * 2 + c).start()
    drains.append(lambda: bulk(COL, 2 * NZ - 1, ssem.at[0]))

    @pl.loop(0, NP)
    def _(b):
        lo = (IDP[pl.ds(pl.multiple_of(b * 8, 8), 8), :] & 255).astype(F32).T
        cols = lax.broadcasted_iota(jnp.int32, (128, 256), 1).astype(F32)
        for i in range(8):
            B[b, pl.ds(i * 128, 128), :] = jnp.where(lo[:, i:i + 1] == cols, 1.0, 0.0).astype(BF16)

    bulk(COL, 2 * NZ - 1, rsem.at[0])
    halves = []
    for h in range(2):
        halves.append(jnp.concatenate(
            [COL[h * NZ + z].astype(F32) for z in range(NZ)], axis=1))
    X[0, y, x] = jnp.concatenate(halves, axis=0).astype(BF16)
    F2 = NZ * CH
    A, Bh = pl.ds(0, F2 // 2), pl.ds(F2 // 2, F2 // 2)

    def on(*where):
        rcopy(X.at[(0,) + where], X.at[(1,) + where], 2, g, sib, rsem.at[2]).start()
    own_a, own_b = X.at[0, y, x, :, A], X.at[0, y, x, :, Bh]
    row_a, col_b = X.at[0, y, :, :, A], X.at[0, :, x, :, Bh]
    own_as, own_bs = X.at[0, y, pl.ds(0, NX - 1), :, A], X.at[0, pl.ds(0, NY - 1), x, :, Bh]
    row_as, col_bs = X.at[0, pl.ds(0, NY - 1), :, :, A], X.at[0, :, pl.ds(0, NX - 1), :, Bh]
    to_x(1, own_a, own_a, own_as)
    to_y(17, own_b, own_b, own_bs)
    land(own_as, rsem.at[1])
    to_y(18, row_a, row_a, row_as, r2y.at[y])
    land(own_bs, rsem.at[17])
    to_x(19, col_b, col_b, col_bs, r2x.at[x])
    on(y, slice(None), slice(None), A)
    on(slice(None), x, slice(None), Bh)

    for cp in loads[n_enc + 1:]:
        cp.wait()
    lo, hi = pl.ds(0, 80), pl.ds(80, 64)
    nx, ny = pl.ds(0, NX - 1), pl.ds(0, NY - 1)
    own_q, own_k, own_ba, own_bb = WQ.at[y, x], WK.at[y, x], WB.at[y, x, lo], WB.at[y, x, hi]
    own_qs, own_ks, own_bas, own_bbs = WQ.at[y, nx], WK.at[ny, x], WB.at[y, nx, lo], WB.at[ny, x, hi]
    row_q, col_k, row_b, col_bb = WQ.at[y], WK.at[:, x], WB.at[y, :, lo], WB.at[:, x, hi]
    row_qs, col_ks, row_bs, col_bbs = WQ.at[ny], WK.at[:, nx], WB.at[ny, :, lo], WB.at[:, nx, hi]
    for j in range(1, max(NX, NY)):
        if j < NY:
            yy = wrap(y + NY - j, NY)
            land(row_a, r2y.at[yy])
            on(yy, slice(None), slice(None), A)
        if j < NX:
            xx = wrap(x + NX - j, NX)
            land(col_b, r2x.at[xx])
            on(slice(None), xx, slice(None), Bh)
    drains.append(lambda: land(X.at[0], ssem.at[2]))
    to_y(9, own_k, own_k, own_ks)
    to_x(8, own_q, own_q, own_qs)
    to_x(16, own_ba, own_ba, own_bas)
    to_y(20, own_bb, own_bb, own_bbs)

    for cp in loads[:n_enc]:
        cp.wait()
    pre = jnp.dot(X[0].reshape(T, F2), E[0], preferred_element_type=F32)
    land(X.at[1], rsem.at[2])
    pre = pre + jnp.dot(X[1].reshape(T, F2), E[1], preferred_element_type=F32)
    act = jnp.maximum(pre + enc_bias[...][None], 0.0).astype(BF16).astype(F32)

    act = act.reshape(NP, 2, 8, 256)
    a0 = act[:, 0].reshape(R8, 256)
    a1 = act[:, 1].reshape(R8, 256)
    rel = IDP[...] - (g * NT + s) * 256
    low = rel & 127
    left = lax.broadcasted_iota(jnp.int32, (R8, 128), 1) < 64

    def pick(h):
        return jnp.where(
            left,
            jnp.take_along_axis(a0[:, h * 128:(h + 1) * 128], low, axis=1),
            jnp.take_along_axis(a1[:, h * 128:(h + 1) * 128], low, axis=1))
    val = jnp.where(rel >= 128, pick(1), pick(0))
    val = jnp.where((rel >= 0) & (rel < 256), val, 0.0)
    VS[...] = val.reshape(NT, 8, 128).astype(BF16)
    first, NB = NT // 2 - 2, NT // 4
    middle = (s >= first) & (s < first + 4)
    part = pl.ds(jnp.where(middle, s - first, 0) * NB, NB)
    for k in range(4):
        @pl.when(s != first + k)
        def _():
            rcopy(VS.at[pl.ds(k * NB, NB)], VR.at[s], 3, g, first + k).start()
    land(own_ks, rsem.at[9])
    to_x(22, col_k, col_k, col_ks)
    land(own_qs, rsem.at[8])
    to_y(21, row_q, row_q, row_qs)

    @pl.when(middle)
    def _():
        VR[s] = VS[part]
        bulk(VR, NT - 1, rsem.at[3])
        VG[part] = jnp.sum(VR[...].astype(F32), axis=0).astype(BF16)
        for j in range(1, NT):
            rcopy(VG.at[part], VG.at[part], 4, g, wrap(s + j, NT)).start()

    def slots(sem, ref):
        @pl.when(middle)
        def _():
            bulk(ref, 3 * NB, sem)

        @pl.when(jnp.logical_not(middle))
        def _():
            bulk(ref, 4 * NB, sem)

    def spread():
        @pl.when(middle)
        def _():
            bulk(VR, NT - 1, ssem.at[4])
    drains.append(lambda: slots(ssem.at[3], VS))
    drains.append(spread)
    slots(rsem.at[4], VG)

    sub = lax.broadcasted_iota(jnp.int32, (8, 128), 0)
    lft = lax.broadcasted_iota(jnp.int32, (8, 128), 1) < 64
    @pl.loop(0, NP, unroll=8 if NP % 8 == 0 else 1)
    def _(b):
        relb = IDP[pl.ds(pl.multiple_of(b * 8, 8), 8), :] - g * (NT * 256)
        vb = VG[b].astype(F32)
        hi = jnp.where(relb < 0, -1, relb >> 8)
        v0 = jnp.where(lft, vb, 0.0)
        v1 = vb - v0
        rows = []
        for h in range(NT):
            for vz in (v0, v1):
                d = jnp.where(hi == h, vz, 0.0)
                rows.append(jnp.concatenate([jnp.where(sub == i, d, 0.0) for i in range(8)], axis=1))
        lhs = jnp.concatenate(rows, axis=0).astype(BF16)
        sel = jnp.dot(lhs, B[b], preferred_element_type=F32).astype(BF16)
        S[:, pl.ds(pl.multiple_of(b * 16, 16), 16), :] = sel.reshape(NT, 16, 256)
    loads[n_enc].wait()
    rec = dot_nt(S[0], DEC[:, 0:256])
    for h in range(1, NT):
        rec = rec + dot_nt(S[h], DEC[:, h * 256:(h + 1) * 256])
    RS[...] = rec.reshape(NP, 16, CH)
    RR[p] = RS[p]
    to_plane(5, lambda q: RS.at[q], RR.at[p], RS)
    bulk(RR, NP - 1, rsem.at[5])
    land(own_bas, rsem.at[16])
    to_y(23, row_b, row_b, row_bs)
    land(own_bbs, rsem.at[20])
    to_x(24, col_bb, col_bb, col_bbs)
    ZS[...] = jnp.sum(RR[...], axis=0)
    zp = (1 - zh) * NP + p
    zc = rcopy(ZS, ZR, 6, zp, s)
    zc.start()
    drains.append(zc.wait_send)
    zc.wait_recv()
    spl = (ZS[...] + ZR[...] + dec_bias[...][None]).astype(BF16)
    SPF[...] = spl.astype(F32).reshape(2, 8, CH)
    SP[s] = spl

    rcopy(SP.at[s], SP.at[s], 10, g, sib, r7b.at[zl]).start()
    for j in range(1, NZ):
        rcopy(SP.at[s], SP.at[s], 7, g, 2 * wrap(zl + j, NZ) + c, r7.at[zl]).start()
    if NZ > 1:
        drains.append(lambda: bulk(SP, NZ - 1, ssem.at[7]))
    drains.append(lambda: bulk(SP, NZ, ssem.at[10]))
    for j in range(1, NZ):
        z = wrap(zl + NZ - j, NZ)
        there = SP.at[2 * z + c]
        pltpu.make_async_copy(there, there, r7.at[z]).wait()
        rcopy(there, there, 10, g, sib, r7b.at[z]).start()
    for z in range(NZ):
        pltpu.make_async_copy(SP.at[0], SP.at[0], r7b.at[z]).wait()

    ss = jnp.zeros((16, 1), F32)
    for j in range(NT):
        xj = SP[j].astype(F32)
        ss = ss + jnp.sum(xj * xj, axis=1, keepdims=True)
    rn = lax.rsqrt(ss / D + EPS)
    normed = []
    for j in range(NH):
        cj = zh * NH + j
        normed.append(SP[cj].astype(F32) * rn * GIN[pl.ds(cj, 1), :])
    normed = jnp.concatenate(normed, axis=1).astype(BF16)
    land(col_ks, rsem.at[22])
    YKS[...] = jnp.dot(normed, WK[...].reshape(NH * CH, 256), preferred_element_type=F32)
    kc = rcopy(YKS, YKR, 11, zp, s)
    kc.start()
    drains.append(kc.wait_send)
    land(row_qs, rsem.at[21])
    YQS[...] = jnp.dot(normed, WQ[...].reshape(NH * CH, 256), preferred_element_type=F32)
    qc = rcopy(YQS, YQR, 25, zp, s)
    qc.start()
    drains.append(qc.wait_send)

    def rot(v):
        return v * cosine + pltpu.roll(v, 64, 1) * sine
    kc.wait_recv()
    kv = YKS[...] + YKR[...]
    KV[p] = jnp.concatenate([rot(kv[:, 0:128]), kv[:, 128:256]], axis=1).astype(BF16)
    to_plane(12, lambda q: KV.at[p], KV.at[p], KV)
    qc.wait_recv()
    qs = YQS[...] + YQR[...]
    QB[...] = jnp.concatenate(
        [rot(qs[:, 0:128]) * QUERY_SCALE, rot(qs[:, 128:256]) * QUERY_SCALE], axis=1).astype(BF16)
    bulk(KV, NP - 1, rsem.at[12])

    kk = KV[:, :, 0:128].reshape(T, 128)
    vv = KV[:, :, 128:256].reshape(T, 128)
    for h in range(2):
        sc = dot_nt(QB[:, h * 128:(h + 1) * 128], kk)
        w = jnp.where(allowed, jnp.exp(SOFT_CAP * jnp.tanh(sc / SOFT_CAP)), 0.0)
        tot = jnp.sum(w, axis=1, keepdims=True)
        mixed = jnp.dot(w.astype(BF16), vv, preferred_element_type=F32)
        HO[:, h * 128:(h + 1) * 128] = (mixed / tot).astype(BF16)
    land(row_bs, rsem.at[23])
    land(col_bbs, rsem.at[24])
    wb = WB[...].reshape(NH * CH, 256)
    for j in range(NH):
        o = dot_nt(HO[...], wb[j * CH:(j + 1) * CH])
        OSD[0, j] = o[:8]
        OSD[1, j] = o[8:]

    oc = rcopy(OSD.at[1 - c], OSR, 13, g, sib)
    oc.start()
    drains.append(oc.wait_send)
    oc.wait_recv()
    OSS[...] = (OSD[c] + OSR[...]).astype(BF16)
    own = (c == zh) & (s // NH == zh)
    for j in range(NH):
        here = (c == zh) & (zh * NH + j == s)

        @pl.when(here)
        def _():
            OR[zl] = OSS[j]

        @pl.when(jnp.logical_not(here))
        def _():
            rcopy(OSS.at[j], OR.at[zl], 14, c * NP + p, zh * NH + j).start()

    def bulk_own(ref, sem):
        @pl.when(own)
        def _():
            if NZ > 1:
                bulk(ref, NZ - 1, sem)

        @pl.when(jnp.logical_not(own))
        def _():
            bulk(ref, NZ, sem)
    drains.append(lambda: bulk_own(OSS, ssem.at[14]))
    bulk_own(OR, rsem.at[14])
    att = jnp.sum(OR[...].astype(F32), axis=0)
    diag = lax.broadcasted_iota(jnp.int32, (8, 128), 0) == lax.broadcasted_iota(jnp.int32, (8, 128), 1)
    NR[s] = jnp.sum(jnp.where(diag, jnp.sum(att * att, axis=1, keepdims=True), 0.0), axis=0, keepdims=True)
    to_tensor(15, lambda q: NR.at[s], NR.at[s], NR)
    bulk(NR, NT - 1, rsem.at[15])
    tot = jnp.sum(jnp.where(diag, jnp.sum(NR[...], axis=0), 0.0), axis=1, keepdims=True)
    post = att * lax.rsqrt(tot / D + EPS) * GPO[pl.ds(s, 1), :]
    out_ref[...] = (SPF[zh] + post).astype(BF16)
    drain()


def local(mesh, resid, enc, enc_bias, ids, dec, dec_bias, segs, gin, gpo, qw, kw, vw, ow):
    NT = mesh.shape["tensor"]
    NP = mesh.shape["dp"] // 2
    assert NT == NP
    T, CH, NZ = 16 * NP, resid.shape[1], NT // 2
    HC = CH // 2
    NX = 1 << (NP.bit_length() // 2)
    NY = NP // NX
    V = pltpu.VMEM
    scratch = [
        V((2, NZ * CH, 256), BF16), V(dec.shape[::-1], BF16), V((NY, NX, HC, 256), BF16),
        V((NY, NX, HC, 256), BF16), V((NY, NX, HC, 256), BF16),
        V((2 * NZ, 8, CH), BF16), V((2, NY, NX, 16, NZ * CH), BF16), V((128, 8 * NP), jnp.int32),
        V((8 * NP, 128), jnp.int32), V((NP, 1024, 256), BF16),
        V((NT, 8, 128), BF16), V((NT, NT // 4, 8, 128), BF16), V((NT, 8, 128), BF16), V((NT, T, 256), BF16),
        V((NP, 16, CH), F32), V((NP, 16, CH), F32), V((16, CH), F32), V((16, CH), F32),
        V((2, 8, CH), F32), V((NT, 16, CH), BF16), V((NT, CH), F32), V((NT, CH), F32),
        V((16, 256), F32), V((16, 256), F32), V((16, 256), F32), V((16, 256), F32), V((16, 256), BF16), V((NP, 16, 256), BF16),
        V((T, 128), F32), V((16, 256), BF16),
        V((2, NZ, 8, CH), F32), V((NZ, 8, CH), F32), V((NZ, 8, CH), BF16), V((NZ, 8, CH), BF16),
        V((NT, 1, 128), F32),
        pltpu.SemaphoreType.DMA((2 * NZ + 5,)), pltpu.SemaphoreType.DMA((26,)),
        pltpu.SemaphoreType.DMA((26,)), pltpu.SemaphoreType.DMA((NX,)), pltpu.SemaphoreType.DMA((NY,)),
        pltpu.SemaphoreType.DMA((NZ,)), pltpu.SemaphoreType.DMA((NZ,)),
    ]
    vm = pl.BlockSpec(memory_space=V)
    hbm = pl.BlockSpec(memory_space=pl.ANY)
    return pl.pallas_call(
        lambda *refs: kernel(NP, NT, NX, NY, *refs),
        out_shape=jax.ShapeDtypeStruct((8, CH), BF16),
        in_specs=[vm, hbm, vm, vm, hbm, vm, vm, vm, vm, hbm, hbm, hbm, hbm],
        out_specs=vm,
        scratch_shapes=scratch,
        compiler_params=pltpu.CompilerParams(
            collective_id=0, has_side_effects=True, vmem_limit_bytes=56 * 1024 * 1024),
    )(resid, enc, enc_bias, ids.T, dec.T, dec_bias, segs, gin, gpo, qw, kw, vw, ow.T)


def solution(mesh):
    return jax.shard_map(
        lambda *args: local(mesh, *args),
        mesh=mesh,
        in_specs=(
            P("dp", "tensor"),
            P(None, ("dp", "tensor")),
            P(("dp", "tensor")),
            P(),
            P("dp", "tensor"),
            P("tensor"),
            P(),
            P(),
            P(),
            P("dp", "tensor"),
            P("dp", "tensor"),
            P("dp", "tensor"),
            P("tensor", "dp"),
        ),
        out_specs=P("dp", "tensor"),
        check_vma=False,
    )
```
